32 devices in a mesh: space: 4 (over z), dir: 4 (over y, x), band: 2 (over core).
Axes of the slice: x: 2, y: 2, z: 4, core: 2. Of those that a mesh axis runs over, the one named last changes fastest.
Arguments:
- adjoint_start: float32 [64, 32, 24, 1152], P('dir', 'band', 'space'), may hold values from 0.5 to 1.5
- primal_deviations: float32 [64, 32, 24, 1152], P('dir', 'band', 'space'), may hold values from 0.5 to 1.5
- density: float32 [24, 1152], P('space'), may hold values from 0 to 1
- material: int32 [24, 1152], P('space'), may hold values from 0 to 3
- rate_table: float32 [4, 32], P(None, 'band'), may hold values from 0.05 to 2
- group_speed: float32 [32], P('band'), may hold values from 0.3 to 3
- heat_capacity: float32 [32], replicated, may hold values from 0.1 to 4, as said below
- objective_weight: float32 [24, 1152], P('space'), may hold values from -6 to 6
Outputs:
- dual_intensity: float32 [64, 32, 24, 1152], P('dir', 'band', 'space')
- design_gradient: float32 [24, 1152], P('space')
The draws below stay inside these ranges and needn't reach their ends.
Inputs may be any that keep to these rules, and one draw needn't show every extreme that they name: `heat_capacity`: heat capacities of the bands, positive.
All inputs are finite; a program needn't handle non-finite values.
Results may differ from the reference program's by a relative error of at most 0.0003.
Values sent between devices are 32-bit elements; how exact they have to be, the bound alone decides.
No kernel may reach another device: no remote copies, remote signals or barrier semaphores. Data moves between devices by JAX's collectives and lax.ppermute only.
A program may use at most 128 MiB of HBM per device.

```python
import math
import jax
import jax.numpy as jnp
from jax import lax

NDIR = 64
NB = 32
NMAT = 4
NY = 192
NZ = 6
ITERS = 2
PLANE = 1152
NX = 24
DIR_DEV = 16


def draw_heat_capacity(key, part):
    index = jnp.arange(NB).astype(jnp.float32)
    factor = jax.random.uniform(key, (NB,), jnp.float32, 0.8, 1.2)
    return 0.3 * jnp.exp(jnp.log(10.0) * index / NB) * factor


def set_ends(drawn, stream_key, least, top_value):
    dims = drawn.shape
    spot = [jax.random.randint(jax.random.fold_in(stream_key, axis), (), 0, dims[axis]) for axis in range(len(dims))]
    drawn = drawn.at[tuple(spot)].set(least)
    longest = dims.index(max(dims))
    spot[longest] = (spot[longest] + 1) % dims[longest]
    return drawn.at[tuple(spot)].set(top_value)


def steps_of(stream_key, dims, cuts, low, high):
    loudness = 1.0
    for dim, shards_of in cuts:
        heights = jax.random.uniform(jax.random.fold_in(jax.random.fold_in(stream_key, 6), dim), (shards_of,), jnp.float32, low / len(cuts), high / len(cuts))
        loudness = loudness * jnp.repeat(jnp.exp(heights), dims[dim] // shards_of).reshape((-1,) + (1,) * (len(dims) - 1 - dim))
    return loudness


def scatter_about(stream_key, dims, scale, most, split=(), kind=jnp.bfloat16):
    result = scale * jax.random.normal(stream_key, dims, jnp.float32)
    if split:
        result = result * steps_of(stream_key, dims, split, -0.22, 0.18)
    return jnp.clip(result, -most, most).astype(kind)


def setup_inputs(seed: int = 0) -> dict:
    keys = jax.random.split(jax.random.key(seed), 9)
    return {
        "adjoint_start": jnp.clip(0.5 + 1.0 * jax.random.uniform(keys[0], (NDIR, NB, NX, PLANE), jnp.float32) ** steps_of(keys[0], (NDIR, NB, NX, PLANE), ((0, 4), (1, 2), (2, 4)), -0.2, 0.2), 0.5, 1.5),
        "primal_deviations": jnp.clip(0.5 + 1.0 * jax.random.uniform(keys[1], (NDIR, NB, NX, PLANE), jnp.float32) ** steps_of(keys[1], (NDIR, NB, NX, PLANE), ((0, 4), (1, 2), (2, 4)), -0.2, 0.2), 0.5, 1.5),
        "density": jnp.clip(1.0 * jax.random.uniform(keys[2], (NX, PLANE), jnp.float32) ** steps_of(keys[2], (NX, PLANE), ((0, 4),), -0.2, 0.2), 0.0, 1.0),
        "material": set_ends(jax.random.randint(keys[3], (NX, PLANE), 0, NMAT), jax.random.fold_in(keys[3], 1), 0, NMAT - 1).astype(jnp.int32),
        "rate_table": jnp.clip(jnp.exp(math.log(2.0) - 3.6888794 * jax.random.uniform(keys[4], (NMAT, NB), jnp.float32) ** steps_of(keys[4], (NMAT, NB), ((1, 2),), -0.2, 0.2)), 0.05, 2.0),
        "group_speed": jnp.clip(jnp.exp(math.log(3.0) - 2.3025851 * jax.random.uniform(keys[5], (NB,), jnp.float32) ** steps_of(keys[5], (NB,), ((0, 2),), -0.2, 0.2)), 0.3, 3.0),
        "heat_capacity": draw_heat_capacity(jax.random.fold_in(keys[8], 71), 0),
        "objective_weight": scatter_about(keys[7], (NX, PLANE), 1.0, 6.0, ((0, 4),), jnp.float32),
    }


def directions():
    index = jnp.arange(NDIR, dtype=jnp.int32)
    half = DIR_DEV // 2
    block = index // DIR_DEV
    slot = index % DIR_DEV
    side = slot // half
    pair = slot % half
    azimuth = jnp.pi * ((block * half + pair).astype(jnp.float32) + 0.5) / (NDIR // 2) - jnp.pi / 2
    along_z = 0.4 * (1.0 - 2.0 * (pair % 2).astype(jnp.float32))
    tilt = jnp.sqrt(1.0 - along_z * along_z)
    along_x = (1.0 - 2.0 * side.astype(jnp.float32)) * tilt * jnp.cos(azimuth)
    along_y = tilt * jnp.sin(azimuth)
    return (along_x, along_y, along_z)

def ahead(field, grid_axis):
    size = field.shape[grid_axis]
    rest = lax.slice_in_dim(field, 1, size, axis=grid_axis)
    return jnp.concatenate([rest, jnp.zeros_like(lax.slice_in_dim(field, 0, 1, axis=grid_axis))], grid_axis)

def behind(field, grid_axis):
    size = field.shape[grid_axis]
    rest = lax.slice_in_dim(field, 0, size - 1, axis=grid_axis)
    return jnp.concatenate([jnp.zeros_like(lax.slice_in_dim(field, 0, 1, axis=grid_axis)), rest], grid_axis)

def plane_move(field, offset):
    last = field.ndim - 1
    size = field.shape[last]
    if offset > 0:
        rest = lax.slice_in_dim(field, offset, size, axis=last)
        pad_block = jnp.zeros_like(lax.slice_in_dim(field, 0, offset, axis=last))
        return jnp.concatenate([rest, pad_block], last)
    rest = lax.slice_in_dim(field, 0, size + offset, axis=last)
    pad_block = jnp.zeros_like(lax.slice_in_dim(field, 0, -offset, axis=last))
    return jnp.concatenate([pad_block, rest], last)

def reference(adjoint_start, primal_deviations, density, material, rate_table, group_speed, heat_capacity, objective_weight):
    along_x, along_y, along_z = directions()
    position = jnp.arange(NZ * NY, dtype=jnp.int32) % NY
    keep_ahead = (position < NY - 1).astype(jnp.float32)
    keep_behind = (position > 0).astype(jnp.float32)
    indicator = (material[None] == jnp.arange(NMAT, dtype=jnp.int32)[:, None, None]).astype(jnp.float32)
    base = jnp.einsum('mb,mxp->bxp', rate_table, indicator, precision=lax.Precision.HIGHEST)
    relaxation_frequency = base * (0.2 + 0.8 * density)[None]
    relaxation_slope = 0.8 * base
    weights = heat_capacity / (NDIR * jnp.sum(heat_capacity))
    column = weights[:, None, None]
    speed = group_speed[:, None, None]

    def thermal_share(spatial_excess):
        return lax.optimization_barrier(jnp.sum(column * spatial_excess, axis=0))

    def relaxation_share(field):
        return lax.optimization_barrier(jnp.sum(relaxation_frequency * field, axis=0))
    crystal_kelvin = lax.optimization_barrier(jnp.sum(lax.map(thermal_share, primal_deviations), axis=0))
    exchange_link = lax.optimization_barrier(jnp.sum(lax.map(relaxation_share, adjoint_start), axis=0))
    cell_source = NDIR * NB * objective_weight
    dual_intensity = adjoint_start
    gradient = jnp.zeros_like(density)
    for step in range(ITERS):
        source = column * (exchange_link + cell_source)[None]

        def one_direction(item):
            comp_x, comp_y, comp_z, field, spatial_excess = item
            speed_x = speed * jnp.abs(comp_x)
            speed_y = speed * jnp.abs(comp_y)
            speed_z = speed * jnp.abs(comp_z)
            near = speed_x * jnp.where(comp_x > 0, ahead(field, 1), behind(field, 1))
            near = near + speed_y * jnp.where(comp_y > 0, plane_move(field, 1) * keep_ahead, plane_move(field, -1) * keep_behind)
            near = near + speed_z * jnp.where(comp_z > 0, plane_move(field, NY), plane_move(field, -NY))
            refreshed_excess = (source + near) / (speed_x + speed_y + speed_z + relaxation_frequency)
            return (refreshed_excess, lax.optimization_barrier(jnp.sum(relaxation_frequency * refreshed_excess, axis=0)), lax.optimization_barrier(jnp.sum(relaxation_slope * refreshed_excess * (spatial_excess - crystal_kelvin[None]), axis=0)))
        dual_intensity, rate_parts, term_parts = lax.map(one_direction, (along_x, along_y, along_z, dual_intensity, primal_deviations))
        exchange_link = lax.optimization_barrier(jnp.sum(rate_parts, axis=0))
        gradient = gradient + lax.optimization_barrier(jnp.sum(term_parts, axis=0))
    return (dual_intensity, gradient * (-0.125 / ITERS))
```

```python
import math

import jax
import jax.numpy as jnp
import numpy as np
from jax import lax
from jax.experimental import pallas as pl
from jax.experimental.pallas import tpu as pltpu
from jax.sharding import PartitionSpec as P

NDIR = 64
NB = 32
NY = 192
ITERS = 2
LANES = 128
SUB = 8
PAIR = 2
VMEM_LIMIT = 40 * 1024 * 1024


def direction_table(count):
    d = np.arange(NDIR)
    half = count // 2
    block, slot = d // count, d % count
    side, pair = slot // half, slot % half
    azimuth = np.pi * (block * half + pair + 0.5) / (NDIR // 2) - np.pi / 2
    along_z = 0.4 * (1.0 - 2.0 * (pair % 2))
    tilt = np.sqrt(1.0 - along_z * along_z)
    along_x = (1.0 - 2.0 * side) * tilt * np.cos(azimuth)
    along_y = tilt * np.sin(azimuth)
    return np.stack([along_x, along_y, along_z], axis=1).astype(np.float32).reshape(-1)


def lane_ids():
    return lax.broadcasted_iota(jnp.int32, (SUB, LANES), 1)


def shift_ahead(v, offset, lane, masked=None):
    n = len(v)
    q, rem = divmod(offset, LANES)
    zero = jnp.zeros((SUB, LANES), jnp.float32)
    rolled = [pltpu.roll(t, LANES - rem, 1) if rem and j >= q else t for j, t in enumerate(v)]
    out = []
    for j in range(n):
        near = rolled[j + q] if j + q < n else None
        far = rolled[j + q + 1] if rem and j + q + 1 < n else None
        bad = [k for k in range(LANES) if masked is not None and masked(j * LANES + k)]
        if rem and far is not None and all(k in bad for k in range(LANES - rem, LANES)):
            far, bad = None, [k for k in bad if k < LANES - rem]
        if near is None:
            out.append(None)
            continue
        t = near
        if rem:
            t = jnp.where(lane < LANES - rem, near, zero if far is None else far)
        for k in bad:
            if not (rem and far is None and k >= LANES - rem):
                t = jnp.where(lane == k, zero, t)
        out.append(t)
    return out


def shift_behind(v, offset, lane, masked=None):
    n = len(v)
    q, rem = divmod(offset, LANES)
    zero = jnp.zeros((SUB, LANES), jnp.float32)
    rolled = [pltpu.roll(t, rem, 1) if rem and j + q < n else t for j, t in enumerate(v)]
    out = []
    for j in range(n):
        near = rolled[j - q] if j - q >= 0 else None
        far = rolled[j - q - 1] if rem and j - q - 1 >= 0 else None
        bad = [k for k in range(LANES) if masked is not None and masked(j * LANES + k)]
        if rem and far is not None and all(k in bad for k in range(rem)):
            far, bad = None, [k for k in bad if k >= rem]
        if near is None:
            out.append(None)
            continue
        t = near
        if rem:
            t = jnp.where(lane >= rem, near, zero if far is None else far)
        for k in bad:
            if not (rem and far is None and k < rem):
                t = jnp.where(lane == k, zero, t)
        out.append(t)
    return out


def shift_y(v, rising, lane):
    if rising:
        return shift_ahead(v, 1, lane, lambda p: p % NY == NY - 1)
    return shift_behind(v, 1, lane, lambda p: p % NY == 0)


def shift_z(v, rising, lane):
    return shift_ahead(v, NY, lane) if rising else shift_behind(v, NY, lane)


def inverse(x):
    r = pl.reciprocal(x, approx=True)
    return r * (2.0 - x * r)


def column(row, offset, n):
    shape = (n, row.shape[1])
    i0 = lax.broadcasted_iota(jnp.int32, shape, 0)
    i1 = lax.broadcasted_iota(jnp.int32, shape, 1)
    picked = jnp.sum(jnp.where(i1 == i0 + offset, row, 0.0), axis=1, keepdims=True)
    return jnp.broadcast_to(picked, (n, LANES))


def fill_columns(cols, heat, speed, table):
    nb = cols.shape[1]
    row = heat[...]
    total = jnp.sum(row, axis=1, keepdims=True) * float(NDIR)
    cols[0] = column(speed[...], 0, nb)
    cols[1] = column(row / total, lax.axis_index("band") * nb, nb)
    for m in range(table.shape[0]):
        cols[2 + m] = column(table[m : m + 1], 0, nb)


def base_tile(cols, material, hs):
    base = jnp.broadcast_to(cols[2, hs], (SUB, LANES))
    for m in range(1, cols.shape[0] - 2):
        base = jnp.where(material == m, cols[2 + m, hs], base)
    return base


def halves(nb):
    return [slice(h * SUB, (h + 1) * SUB) for h in range(nb // SUB)]


def tiles(plane):
    return [slice(j * LANES, (j + 1) * LANES) for j in range(plane // LANES)]


def sub_sum(t):
    return jnp.sum(t, axis=0, keepdims=True)


def add_terms(terms):
    terms = [t for t in terms if t is not None]
    total = terms[0]
    for t in terms[1:]:
        total = total + t
    return total


def times(a, b):
    return None if b is None else a * b


def cosines(dirs, d):
    at = 3 * d
    return dirs[at], dirs[at + 1], dirs[at + 2]


def faces_kernel(heat, speed, table, density, material, objective, up0, down0, down1, up1, out_ahead, out_behind, cols):
    fill_columns(cols, heat, speed, table)
    half, _, nb, plane = up0.shape
    last = density.shape[0] - 1
    for own, other, x, out in ((up0, down0, 0, out_ahead), (down1, up1, last, out_behind)):

        def copy(d, total):
            out[pl.ds(pl.multiple_of(d * nb, nb), nb)] = own[d, 0]
            return total + (own[d, 0] + other[d, 0])

        total = lax.fori_loop(0, half, copy, jnp.zeros((nb, plane), jnp.float32))
        base = half * nb
        for cs in tiles(plane):
            share = 0.0
            for hs in halves(nb):
                rate = base_tile(cols, material[x : x + 1, cs], hs) * (0.2 + 0.8 * density[x : x + 1, cs])
                share = share + rate * total[hs, cs]
            out[base : base + 1, cs] = sub_sum(share)
        out[base + 1 : base + 2] = density[x : x + 1]
        out[base + 2 : base + 3] = material[x : x + 1].astype(jnp.float32)
        out[base + 3 : base + 4] = objective[x : x + 1]
        out[base + 4 : base + 8] = jnp.zeros((4, plane), jnp.float32)


def first_kernel(
    dirs, heat, speed, table, density, material, field, excess, flow, face_ahead, face_behind, sums, cols, rate, acc
):
    g = pl.program_id(0)
    steps = pl.num_programs(0)
    _, nx, nb, plane = field.shape
    cuts, bands = tiles(plane), halves(nb)

    @pl.when(g == 0)
    def _():
        fill_columns(cols, heat, speed, table)
        for x in range(nx):
            for cs in cuts:
                factor = 0.2 + 0.8 * density[x : x + 1, cs]
                for hs in bands:
                    rate[x, hs, cs] = base_tile(cols, material[x : x + 1, cs], hs) * factor
        acc[...] = jnp.zeros_like(acc)

    block = lax.axis_index("dir")
    count = steps * PAIR
    first = block * count + g * PAIR
    ahead = g < steps // 2
    lane = lane_ids()

    def run(rising):
        def layer(x, _):
            edge = jnp.where(ahead, x == nx - 1, x == 0)
            beside = jnp.where(edge, x, jnp.where(ahead, x + 1, x - 1))
            for hs in bands:
                pace = cols[0, hs]
                rates = [rate[x, hs, cs] for cs in cuts]
                kept = [[] for _ in cuts]
                for dd in range(PAIR):
                    ax, ay, az = [jnp.abs(a) for a in cosines(dirs, first + dd)]
                    cx, cy, cz = pace * jnp.where(edge, 0.0, ax), pace * ay, pace * az
                    speeds = pace * (ax + ay + az)
                    v = [field[dd, x, hs, cs] for cs in cuts]
                    along_y = shift_y(v, rising, lane)
                    along_z = shift_z(v, dd == 0, lane)
                    for j, cs in enumerate(cuts):
                        inv = inverse(speeds + rates[j])
                        near = add_terms(
                            [times(cx, field[dd, beside, hs, cs]), times(cy, along_y[j]), times(cz, along_z[j])]
                        )
                        a = near * inv
                        flow[dd, x, hs, cs] = a
                        kept[j].append((v[j], excess[dd, x, hs, cs], a, inv))
                for j, cs in enumerate(cuts):
                    for f in range(4):
                        acc[f, x, hs, cs] += add_terms([k[f] for k in kept[j]])
            return 0

        lax.fori_loop(0, nx, layer, 0)

    rises = cosines(dirs, first)[1] > 0
    pl.when(rises)(lambda: run(True))
    pl.when(jnp.logical_not(rises))(lambda: run(False))

    @pl.when(ahead)
    def _():
        for dd in range(PAIR):
            face_ahead[dd * nb : (dd + 1) * nb] = flow[dd, 0]

    @pl.when(jnp.logical_not(ahead))
    def _():
        for dd in range(PAIR):
            face_behind[dd * nb : (dd + 1) * nb] = flow[dd, nx - 1]

    @pl.when(g == steps - 1)
    def _():
        for x in range(nx):
            for cs in cuts:
                totals = [0.0] * 4
                for hs in bands:
                    r, w = rate[x, hs, cs], cols[1, hs]
                    for f, scale in enumerate((r, w, r, r * w)):
                        totals[f] = totals[f] + scale * acc[f, x, hs, cs]
                for f in range(4):
                    sums[f * nx + x : f * nx + x + 1, cs] = sub_sum(totals[f])
        sums[4 * nx :] = jnp.zeros((sums.shape[0] - 4 * nx, plane), jnp.float32)


def edges_kernel(dirs, heat, speed, table, density, material, from_ahead, from_behind, sums, out, cols):
    fill_columns(cols, heat, speed, table)
    nx, plane = density.shape
    nb = cols.shape[1]
    half = (from_ahead.shape[0] - SUB) // nb
    count = 2 * half
    block = lax.axis_index("dir")
    out[...] = sums[...]
    cuts = tiles(plane)
    for side, (halo, x) in enumerate(((from_ahead, nx - 1), (from_behind, 0))):
        rates = []
        for hs in halves(nb):
            rates.append(
                [base_tile(cols, material[x : x + 1, cs], hs) * (0.2 + 0.8 * density[x : x + 1, cs]) for cs in cuts]
            )

        def add(d, totals):
            ax, ay, az = [jnp.abs(a) for a in cosines(dirs, block * count + side * half + d)]
            new = list(totals)
            for h, hs in enumerate(halves(nb)):
                pace = cols[0, hs]
                cx, speeds = pace * ax, pace * (ax + ay + az)
                rows = halo.at[pl.ds(pl.multiple_of(d * nb + h * SUB, SUB), SUB)]
                for j, cs in enumerate(cuts):
                    r = rates[h][j]
                    new[j] = new[j] + (cx * rows[:, cs]) * (r * inverse(speeds + r))
            return tuple(new)

        totals = lax.fori_loop(0, half, add, tuple(jnp.zeros((SUB, LANES), jnp.float32) for _ in cuts))
        row = 2 * nx + x
        for j, cs in enumerate(cuts):
            out[row : row + 1, cs] = out[row : row + 1, cs] + sub_sum(totals[j])
        out[4 * nx + side : 4 * nx + side + 1] = halo[half * nb : half * nb + 1]


def second_kernel(
    dirs, heat, speed, table, density, material, objective,
    sum0, sum1, sum2, sum3, params_ahead, params_behind, halo0_ahead, halo0_behind, halo1_ahead, halo1_behind,
    flow, excess, dual, gradient,
    cols, rate, source0, source1, warm, prev, seed, acc,
):
    g = pl.program_id(0)
    steps = pl.num_programs(0)
    _, nx, nb, plane = flow.shape
    cuts, bands = tiles(plane), halves(nb)
    scale = float(NDIR * NB)

    @pl.when(g == 0)
    def _():
        fill_columns(cols, heat, speed, table)
        total = (sum0[...] + sum1[...]) + (sum2[...] + sum3[...])
        for x in range(nx):
            warm[x] = jnp.broadcast_to(total[nx + x : nx + x + 1], (SUB, plane))
        for x in range(nx + 2):
            for cs in cuts:
                if x < nx:
                    dens, mat = density[x : x + 1, cs], material[x : x + 1, cs]
                    drive = total[x : x + 1, cs] + scale * objective[x : x + 1, cs]
                    again = (
                        total[2 * nx + x : 2 * nx + x + 1, cs]
                        + drive * total[3 * nx + x : 3 * nx + x + 1, cs]
                        + scale * objective[x : x + 1, cs]
                    )
                else:
                    params = params_ahead if x == nx else params_behind
                    dens, mat = params[1:2, cs], params[2:3, cs].astype(jnp.int32)
                    drive = total[3 * nx + x : 3 * nx + x + 1, cs] + scale * params[3:4, cs]
                factor = 0.2 + 0.8 * dens
                for hs in bands:
                    w = cols[1, hs]
                    rate[x, hs, cs] = base_tile(cols, mat, hs) * factor
                    source0[x, hs, cs] = w * drive
                    if x < nx:
                        source1[x, hs, cs] = w * again
        acc[...] = jnp.zeros_like(acc)

    block = lax.axis_index("dir")
    count = steps * PAIR
    first = block * count + g * PAIR
    ahead = g < steps // 2
    lane = lane_ids()

    def enter(halo0, halo1, x):
        for dd in range(PAIR):
            ax, ay, az = [jnp.abs(a) for a in cosines(dirs, first + dd)]
            for h, hs in enumerate(bands):
                pace = cols[0, hs]
                speeds, cx = pace * (ax + ay + az), pace * ax
                rows = slice(dd * nb + h * SUB, dd * nb + (h + 1) * SUB)
                for cs in cuts:
                    prev[dd, hs, cs] = halo1[rows, cs] + source0[x, hs, cs] * inverse(speeds + rate[x, hs, cs])
                    seed[dd, hs, cs] = cx * halo0[rows, cs]

    pl.when(ahead)(lambda: enter(halo0_ahead, halo1_ahead, nx))
    pl.when(jnp.logical_not(ahead))(lambda: enter(halo0_behind, halo1_behind, nx + 1))

    def run(rising):
        def layer(i, at_edge):
            x = jnp.where(ahead, nx - 1 - i, i)
            for hs in bands:
                pace = cols[0, hs]
                rates = [rate[x, hs, cs] for cs in cuts]
                kept = [[] for _ in cuts]
                for dd in range(PAIR):
                    ax, ay, az = [jnp.abs(a) for a in cosines(dirs, first + dd)]
                    cx, cy, cz = pace * ax, pace * ay, pace * az
                    speeds = pace * (ax + ay + az)
                    inv = [inverse(speeds + rates[j]) for j in range(len(cuts))]
                    v = []
                    for j, cs in enumerate(cuts):
                        s = source0[x, hs, cs]
                        if at_edge:
                            s = s + seed[dd, hs, cs]
                        v.append(flow[dd, x, hs, cs] + s * inv[j])
                    along_y = shift_y(v, rising, lane)
                    along_z = shift_z(v, dd == 0, lane)
                    for j, cs in enumerate(cuts):
                        near = add_terms([
                            times(cx, prev[dd, hs, cs]), times(cy, along_y[j]), times(cz, along_z[j]), source1[x, hs, cs]
                        ])
                        new = near * inv[j]
                        prev[dd, hs, cs] = v[j]
                        dual[dd, x, hs, cs] = new
                        kept[j].append((v[j] + new) * (excess[dd, x, hs, cs] - warm[x, :, cs]))
                for j, cs in enumerate(cuts):
                    acc[x, hs, cs] += add_terms(kept[j])

        layer(0, True)

        def later(i, _):
            layer(i, False)
            return 0

        lax.fori_loop(1, nx, later, 0)

    rises = cosines(dirs, first)[1] > 0
    pl.when(rises)(lambda: run(True))
    pl.when(jnp.logical_not(rises))(lambda: run(False))

    @pl.when(g == steps - 1)
    def _():
        for x in range(nx):
            for cs in cuts:
                total = 0.0
                for hs in bands:
                    total = total + base_tile(cols, material[x : x + 1, cs], hs) * acc[x, hs, cs]
                gradient[x : x + 1, cs] = sub_sum(total) * 0.8


def passed_along(value, steps):
    count = lax.axis_size("space")
    return lax.ppermute(value, "space", [(s, s + steps) for s in range(count) if 0 <= s + steps < count])


def shares(partial):
    size = lax.axis_size("band")
    total = partial
    for k in range(1, size):
        total = total + lax.ppermute(partial, "band", [(s, (s + k) % size) for s in range(size)])
    count = lax.axis_size("dir")
    pairs = count & (count - 1) == 0
    hops = [[(s, s ^ k if pairs else (s + k) % count) for s in range(count)] for k in range(1, count)]
    return [total] + [lax.ppermute(total, "dir", hop) for hop in hops]


def whole(array):
    return pl.BlockSpec(array.shape, lambda *g: (0,) * array.ndim)


def on_device(
    adjoint_start, primal_deviations, density, material, rate_table, group_speed, heat_capacity, objective_weight
):
    count, nb, nx, plane = adjoint_start.shape
    half = count // 2
    steps = count // PAIR
    nmat = rate_table.shape[0]
    start = adjoint_start.transpose(0, 2, 1, 3)
    excess = primal_deviations.transpose(0, 2, 1, 3)
    f32 = jnp.float32
    smem = pl.BlockSpec(memory_space=pltpu.SMEM)
    dirs = jnp.asarray(direction_table(count))
    heat = heat_capacity.reshape(1, -1)
    speed = group_speed.reshape(1, -1)
    tables = (heat, speed, rate_table)
    cells = (density, material)
    cols = pltpu.VMEM((2 + nmat, nb, LANES), f32)
    params = pltpu.CompilerParams(vmem_limit_bytes=VMEM_LIMIT)
    size = count * nb * nx * plane

    def face(d, x):
        return pl.BlockSpec((half, 1, nb, plane), lambda g: (d, x, 0, 0))

    rows = half * nb + SUB
    small = (*tables, *cells, objective_weight)
    to_behind, to_ahead = pl.pallas_call(
        faces_kernel,
        grid=(1,),
        out_shape=(jax.ShapeDtypeStruct((rows, plane), f32),) * 2,
        in_specs=[whole(a) for a in small] + [face(0, 0), face(1, 0), face(1, nx - 1), face(0, nx - 1)],
        out_specs=[pl.BlockSpec((rows, plane), lambda g: (0, 0))] * 2,
        scratch_shapes=[cols],
        compiler_params=params,
        cost_estimate=pl.CostEstimate(flops=size // 3, bytes_accessed=size * 2, transcendentals=0),
        name="faces",
    )(*small, start, start, start, start)
    halo0_ahead = passed_along(to_behind, -1)
    halo0_behind = passed_along(to_ahead, 1)

    group = pl.BlockSpec((PAIR, nx, nb, plane), lambda g: (g, 0, 0, 0))
    early = pl.BlockSpec((PAIR * nb, plane), lambda g: (jnp.minimum(g, steps // 2 - 1), 0))
    late = pl.BlockSpec((PAIR * nb, plane), lambda g: (jnp.maximum(g - steps // 2, 0), 0))
    sum_rows = -(-(4 * nx + 2) // SUB) * SUB
    small = (*tables, *cells)
    flow, face_ahead, face_behind, sums = pl.pallas_call(
        first_kernel,
        grid=(steps,),
        out_shape=(
            jax.ShapeDtypeStruct(start.shape, f32),
            jax.ShapeDtypeStruct((half * nb, plane), f32),
            jax.ShapeDtypeStruct((half * nb, plane), f32),
            jax.ShapeDtypeStruct((sum_rows, plane), f32),
        ),
        in_specs=[smem] + [whole(a) for a in small] + [group, group],
        out_specs=[group, early, late, pl.BlockSpec((sum_rows, plane), lambda g: (0, 0))],
        scratch_shapes=[cols, pltpu.VMEM((nx, nb, plane), f32), pltpu.VMEM((4, nx, nb, plane), f32)],
        compiler_params=params,
        cost_estimate=pl.CostEstimate(flops=size * 20, bytes_accessed=size * 12, transcendentals=size),
        name="first",
    )(dirs, *small, start, excess)
    halo1_ahead = passed_along(face_ahead, -1)
    halo1_behind = passed_along(face_behind, 1)

    sums = pl.pallas_call(
        edges_kernel,
        out_shape=jax.ShapeDtypeStruct(sums.shape, f32),
        in_specs=[smem] + [pl.BlockSpec(memory_space=pltpu.VMEM)] * (len(small) + 3),
        out_specs=pl.BlockSpec(memory_space=pltpu.VMEM),
        scratch_shapes=[cols],
        compiler_params=params,
        cost_estimate=pl.CostEstimate(flops=size, bytes_accessed=size, transcendentals=0),
        name="edges",
    )(dirs, *small, halo0_ahead, halo0_behind, sums)
    parts = shares(sums)
    parts = parts[:3] + [sum(parts[3:], jnp.zeros_like(sums))] if len(parts) > 4 else parts + [jnp.zeros_like(sums)] * (4 - len(parts))

    small = (*tables, *cells, objective_weight, *parts)
    tail = pl.BlockSpec((SUB, plane), lambda g: (half * nb // SUB, 0))
    dual, gradient = pl.pallas_call(
        second_kernel,
        grid=(steps,),
        out_shape=(jax.ShapeDtypeStruct(start.shape, f32), jax.ShapeDtypeStruct((nx, plane), f32)),
        in_specs=[smem] + [whole(a) for a in small] + [tail, tail, early, late, early, late, group, group],
        out_specs=[group, pl.BlockSpec((nx, plane), lambda g: (0, 0))],
        scratch_shapes=[
            cols,
            pltpu.VMEM((nx + 2, nb, plane), f32),
            pltpu.VMEM((nx + 2, nb, plane), f32),
            pltpu.VMEM((nx, nb, plane), f32),
            pltpu.VMEM((nx, SUB, plane), f32),
            pltpu.VMEM((PAIR, nb, plane), f32),
            pltpu.VMEM((PAIR, nb, plane), f32),
            pltpu.VMEM((nx, nb, plane), f32),
        ],
        compiler_params=params,
        cost_estimate=pl.CostEstimate(flops=size * 30, bytes_accessed=size * 12, transcendentals=size),
        name="second",
    )(dirs, *small, halo0_ahead, halo0_behind, halo0_ahead, halo0_behind, halo1_ahead, halo1_behind, flow, excess)
    gradient = sum(shares(gradient)) * (-0.125 / ITERS)
    return (dual.transpose(0, 2, 1, 3), gradient)


def solution(mesh):
    placed = (
        P("dir", "band", "space", None),
        P("dir", "band", "space", None),
        P("space", None),
        P("space", None),
        P(None, "band"),
        P("band"),
        P(),
        P("space", None),
    )
    return jax.shard_map(
        on_device,
        mesh=mesh,
        in_specs=placed,
        out_specs=(P("dir", "band", "space", None), P("space", None)),
        check_vma=False,
    )
```

```python
import math

import jax
import jax.numpy as jnp
import numpy as np
from jax import lax
from jax.experimental import pallas as pl
from jax.experimental.pallas import tpu as pltpu
from jax.sharding import PartitionSpec as P

NDIR = 64
NB = 32
NY = 192
ITERS = 2
LANES = 128
SUB = 8
FIRST_GROUP = 8
SECOND_GROUP = 4
VMEM_LIMIT = 24 * 1024 * 1024


def direction_table(count):
    d = np.arange(NDIR)
    half = count // 2
    block, slot = d // count, d % count
    side, pair = slot // half, slot % half
    azimuth = np.pi * (block * half + pair + 0.5) / (NDIR // 2) - np.pi / 2
    along_z = 0.4 * (1.0 - 2.0 * (pair % 2))
    tilt = np.sqrt(1.0 - along_z * along_z)
    along_x = (1.0 - 2.0 * side) * tilt * np.cos(azimuth)
    along_y = tilt * np.sin(azimuth)
    return np.stack([along_x, along_y, along_z], axis=1).astype(np.float32).reshape(-1)


def lane_ids():
    return lax.broadcasted_iota(jnp.int32, (SUB, LANES), 1)


def lazily(make):
    made = {}

    def get(j):
        if j not in made:
            made[j] = make(j)
        return made[j]

    return get


def shifted(v, n, offset, lane, masked=None):
    q, rem = divmod(offset, LANES)
    zero = jnp.zeros((SUB, LANES), jnp.float32)
    rolled = lazily(lambda j: pltpu.roll(v(j), LANES - rem, 1) if rem else v(j))

    def tile(j):
        parts = []
        for k, low, high in ((j + q, 0, LANES - rem), (j + q + 1, LANES - rem, LANES)):
            kept = low < high and 0 <= k < n
            kept = kept and not all(masked is not None and masked(j * LANES + i) for i in range(low, high))
            parts.append(rolled(k) if kept else None)
        if parts[0] is None and parts[1] is None:
            return None
        t = parts[0]
        if rem:
            t = jnp.where(lane < LANES - rem, *[zero if part is None else part for part in parts])
        for i in range(LANES):
            if masked is not None and masked(j * LANES + i) and parts[int(i >= LANES - rem)] is not None:
                t = jnp.where(lane == i, zero, t)
        return t

    return lazily(tile)


def shift_y(v, n, rising, lane):
    if rising:
        return shifted(v, n, 1, lane, lambda p: p % NY == NY - 1)
    return shifted(v, n, -1, lane, lambda p: p % NY == 0)


def shift_z(v, n, rising, lane):
    return shifted(v, n, NY if rising else -NY, lane)


def inverse(x):
    r = pl.reciprocal(x, approx=True)
    return r * (2.0 - x * r)


def column(row, offset, n):
    shape = (n, row.shape[1])
    i0 = lax.broadcasted_iota(jnp.int32, shape, 0)
    i1 = lax.broadcasted_iota(jnp.int32, shape, 1)
    picked = jnp.sum(jnp.where(i1 == i0 + offset, row, 0.0), axis=1, keepdims=True)
    return jnp.broadcast_to(picked, (n, LANES))


def fill_columns(cols, heat, speed, table):
    nb = cols.shape[1]
    row = heat[...]
    total = jnp.sum(row, axis=1, keepdims=True) * float(NDIR)
    cols[0] = column(speed[...], 0, nb)
    cols[1] = column(row / total, lax.axis_index("band") * nb, nb)
    for m in range(table.shape[0]):
        cols[2 + m] = column(table[m : m + 1], 0, nb)


def base_tile(cols, material, hs):
    base = jnp.broadcast_to(cols[2, hs], (SUB, LANES))
    for m in range(1, cols.shape[0] - 2):
        base = jnp.where(material == m, cols[2 + m, hs], base)
    return base


def halves(nb):
    return [slice(h * SUB, (h + 1) * SUB) for h in range(nb // SUB)]


def tiles(plane):
    return [slice(j * LANES, (j + 1) * LANES) for j in range(plane // LANES)]


def sub_sum(t):
    return jnp.sum(t, axis=0, keepdims=True)


def add_terms(terms):
    terms = [t for t in terms if t is not None]
    total = terms[0]
    for t in terms[1:]:
        total = total + t
    return total


def times(a, b):
    return None if b is None else a * b


def cosines(dirs, d):
    at = 3 * d
    return dirs[at], dirs[at + 1], dirs[at + 2]


def is_even():
    return lax.axis_index("space") % 2 == 0


def faces_kernel(table_in, density_in, material_in, objective_in, start, out_a, out_b, table, density, material, objective, others, cols, sems):
    half, nb, plane = others.shape[1:]
    last = density.shape[0] - 1
    even = is_even()
    copies = []
    for n, (src, dst) in enumerate(
        ((table_in, table), (density_in, density), (material_in, material), (objective_in, objective))
    ):
        copies.append(pltpu.make_async_copy(src, dst, sems.at[n]))
    for side, out in enumerate((out_a, out_b)):
        upper = even if side == 0 else jnp.logical_not(even)
        first, second, x = jnp.where(upper, half, 0), jnp.where(upper, 0, half), jnp.where(upper, last, 0)
        at = 4 + side * (half + 1)
        for d in range(half):
            copies.append(
                pltpu.make_async_copy(start.at[first + d, x], out.at[pl.ds(d * nb, nb)], sems.at[at + d])
            )
        copies.append(pltpu.make_async_copy(start.at[pl.ds(second, half), x], others.at[side], sems.at[at + half]))
    for copy in copies:
        copy.start()
    for copy in copies:
        copy.wait()
    for m in range(table.shape[0]):
        cols[2 + m] = column(table[m : m + 1], 0, nb)
    for side, out in enumerate((out_a, out_b)):
        upper = even if side == 0 else jnp.logical_not(even)
        row = lambda ref, cs: jnp.where(upper, ref[last : last + 1, cs], ref[0:1, cs])
        base = half * nb
        for cs in tiles(plane):
            dens, mat = row(density, cs), row(material, cs)
            share = 0.0
            for h, hs in enumerate(halves(nb)):
                total = others[side, 0, hs, cs]
                for d in range(1, half):
                    total = total + others[side, d, hs, cs]
                for d in range(half):
                    total = total + out[d * nb + h * SUB : d * nb + (h + 1) * SUB, cs]
                share = share + base_tile(cols, mat, hs) * (0.2 + 0.8 * dens) * total
            out[base : base + 1, cs] = sub_sum(share)
            out[base + 1 : base + 2, cs] = dens
            out[base + 2 : base + 3, cs] = mat.astype(jnp.float32)
            out[base + 3 : base + 4, cs] = row(objective, cs)
            out[base + 4 : base + 8, cs] = jnp.zeros((4, LANES), jnp.float32)


def first_kernel(
    dirs, heat, speed, table, density, material, field, excess, flow, face_a, face_b, sums, cols, rate, acc
):
    g = pl.program_id(0)
    steps = pl.num_programs(0)
    count, nx, nb, plane = field.shape
    per = count // steps
    cuts, bands = tiles(plane), halves(nb)
    n = len(cuts)

    @pl.when(g == 0)
    def _():
        fill_columns(cols, heat, speed, table)
        for x in range(nx):
            for cs in cuts:
                factor = 0.2 + 0.8 * density[x : x + 1, cs]
                for hs in bands:
                    rate[x, hs, cs] = base_tile(cols, material[x : x + 1, cs], hs) * factor
        acc[...] = jnp.zeros_like(acc)

    block = lax.axis_index("dir")
    first = block * count + g * per
    ahead = g < steps // 2
    lane = lane_ids()

    def run(rising):
        def layer(x, _):
            edge = jnp.where(ahead, x == nx - 1, x == 0)
            beside = jnp.where(edge, x, jnp.where(ahead, x + 1, x - 1))
            for hs in bands:
                pace = cols[0, hs]
                ways = []
                for dd in range(per):
                    ax, ay, az = [jnp.abs(a) for a in cosines(dirs, first + dd)]
                    v = lazily(lambda j, dd=dd: field[g * per + dd, x, hs, cuts[j]])
                    speeds = (pace * jnp.where(edge, 0.0, ax), pace * ay, pace * az, pace * (ax + ay + az))
                    ways.append((v, shift_y(v, n, rising, lane), shift_z(v, n, dd % 2 == 0, lane), speeds))
                for j, cs in enumerate(cuts):
                    r = rate[x, hs, cs]
                    kept = []
                    for dd, (v, along_y, along_z, (cx, cy, cz, speeds)) in enumerate(ways):
                        d = g * per + dd
                        inv = inverse(speeds + r)
                        a = inv * add_terms(
                            [times(cx, field[d, beside, hs, cs]), times(cy, along_y(j)), times(cz, along_z(j))]
                        )
                        flow[d, x, hs, cs] = a
                        kept.append((v(j), excess[d, x, hs, cs], a, inv))
                    for f in range(4):
                        acc[f, x, hs, cs] += add_terms([k[f] for k in kept])
            return 0

        lax.fori_loop(0, nx, layer, 0)

    rises = cosines(dirs, first)[1] > 0
    pl.when(rises)(lambda: run(True))
    pl.when(jnp.logical_not(rises))(lambda: run(False))

    def give(face):
        x = jnp.where(ahead, 0, nx - 1)
        skip = jnp.where(ahead, 0, steps // 2)
        for dd in range(per):
            face[pl.ds(pl.multiple_of(((g - skip) * per + dd) * nb, nb), nb)] = flow[g * per + dd, x]

    pl.when(ahead != is_even())(lambda: give(face_a))
    pl.when(ahead == is_even())(lambda: give(face_b))

    @pl.when(g == steps - 1)
    def _():
        for x in range(nx):
            for cs in cuts:
                totals = [0.0] * 4
                for hs in bands:
                    r, w = rate[x, hs, cs], cols[1, hs]
                    for f, scale in enumerate((r, w, r, r * w)):
                        totals[f] = totals[f] + scale * acc[f, x, hs, cs]
                for f in range(4):
                    sums[f * nx + x : f * nx + x + 1, cs] = sub_sum(totals[f])
        sums[4 * nx :] = jnp.zeros((sums.shape[0] - 4 * nx, plane), jnp.float32)


def edges_kernel(dirs, heat, speed, table, density, material, halo_a, halo_b, sums, out, cols):
    fill_columns(cols, heat, speed, table)
    nx, plane = density.shape
    nb = cols.shape[1]
    half = (halo_a.shape[0] - SUB) // nb
    count = 2 * half
    block = lax.axis_index("dir")
    even = is_even()
    out[...] = sums[...]
    cuts = tiles(plane)
    gains = []
    for side, halo in enumerate((halo_a, halo_b)):
        ahead = even if side == 0 else jnp.logical_not(even)
        rates = []
        for hs in halves(nb):
            rates.append([])
            for cs in cuts:
                mat = jnp.where(ahead, material[nx - 1 : nx, cs], material[0:1, cs])
                dens = jnp.where(ahead, density[nx - 1 : nx, cs], density[0:1, cs])
                rates[-1].append(base_tile(cols, mat, hs) * (0.2 + 0.8 * dens))
        first = block * count + jnp.where(ahead, 0, half)

        def add(d, totals):
            ax, ay, az = [jnp.abs(a) for a in cosines(dirs, first + d)]
            new = list(totals)
            for h, hs in enumerate(halves(nb)):
                pace = cols[0, hs]
                cx, speeds = pace * ax, pace * (ax + ay + az)
                rows = halo.at[pl.ds(pl.multiple_of(d * nb + h * SUB, SUB), SUB)]
                for j, cs in enumerate(cuts):
                    r = rates[h][j]
                    new[j] = new[j] + (cx * rows[:, cs]) * (r * inverse(speeds + r))
            return tuple(new)

        totals = lax.fori_loop(0, half, add, tuple(jnp.zeros((SUB, LANES), jnp.float32) for _ in cuts))
        gains.append([sub_sum(t) for t in totals])
    base = half * nb
    for side, x in enumerate((nx - 1, 0)):
        near, far = (0, 1) if side == 0 else (1, 0)
        row = 2 * nx + x
        for j, cs in enumerate(cuts):
            out[row : row + 1, cs] = out[row : row + 1, cs] + jnp.where(even, gains[near][j], gains[far][j])
            a, b = halo_a[base : base + 1, cs], halo_b[base : base + 1, cs]
            out[4 * nx + side : 4 * nx + side + 1, cs] = jnp.where(even, a, b) if side == 0 else jnp.where(even, b, a)


def second_kernel(
    dirs, heat, speed, table, density, material, objective,
    sum0, sum1, sum2, sum3, halo0_a, halo0_b, halo1_a, halo1_b,
    flow, excess, dual, gradient,
    cols, rate, source0, source1, warm, prev, seed, acc,
):
    g = pl.program_id(0)
    steps = pl.num_programs(0)
    count, nx, nb, plane = flow.shape
    per = count // steps
    cuts, bands = tiles(plane), halves(nb)
    n = len(cuts)
    scale = float(NDIR * NB)
    edge = halo0_a.shape[0] - SUB

    @pl.when(g == 0)
    def _():
        fill_columns(cols, heat, speed, table)
        total = (sum0[...] + sum1[...]) + (sum2[...] + sum3[...])
        for x in range(nx):
            warm[x] = jnp.broadcast_to(total[nx + x : nx + x + 1], (SUB, plane))
        for x in range(nx + 2):
            for cs in cuts:
                if x < nx:
                    dens, mat = density[x : x + 1, cs], material[x : x + 1, cs]
                    drive = total[x : x + 1, cs] + scale * objective[x : x + 1, cs]
                    again = (
                        total[2 * nx + x : 2 * nx + x + 1, cs]
                        + drive * total[3 * nx + x : 3 * nx + x + 1, cs]
                        + scale * objective[x : x + 1, cs]
                    )
                else:
                    from_a = is_even() if x == nx else jnp.logical_not(is_even())
                    dens, mat, aim = [
                        jnp.where(from_a, halo0_a[edge + k : edge + k + 1, cs], halo0_b[edge + k : edge + k + 1, cs])
                        for k in (1, 2, 3)
                    ]
                    mat = mat.astype(jnp.int32)
                    drive = total[3 * nx + x : 3 * nx + x + 1, cs] + scale * aim
                factor = 0.2 + 0.8 * dens
                for hs in bands:
                    w = cols[1, hs]
                    rate[x, hs, cs] = base_tile(cols, mat, hs) * factor
                    source0[x, hs, cs] = w * drive
                    if x < nx:
                        source1[x, hs, cs] = w * again
        acc[...] = jnp.zeros_like(acc)

    block = lax.axis_index("dir")
    first = block * count + g * per
    ahead = g < steps // 2
    lane = lane_ids()

    def enter(halo0, halo1):
        x = jnp.where(ahead, nx, nx + 1)
        skip = jnp.where(ahead, 0, steps // 2)
        for dd in range(per):
            ax, ay, az = [jnp.abs(a) for a in cosines(dirs, first + dd)]
            for h, hs in enumerate(bands):
                pace = cols[0, hs]
                speeds, cx = pace * (ax + ay + az), pace * ax
                rows = pl.ds(pl.multiple_of(((g - skip) * per + dd) * nb + h * SUB, SUB), SUB)
                for cs in cuts:
                    prev[dd, hs, cs] = halo1[rows, cs] + source0[x, hs, cs] * inverse(speeds + rate[x, hs, cs])
                    seed[dd, hs, cs] = cx * halo0[rows, cs]

    pl.when(ahead == is_even())(lambda: enter(halo0_a, halo1_a))
    pl.when(ahead != is_even())(lambda: enter(halo0_b, halo1_b))

    def run(rising):
        def layer(i, at_edge):
            x = jnp.where(ahead, nx - 1 - i, i)
            for hs in bands:
                pace = cols[0, hs]
                rates = lazily(lambda j: rate[x, hs, cuts[j]])
                sources = lazily(lambda j: source0[x, hs, cuts[j]])
                ways = []
                for dd in range(per):
                    ax, ay, az = [jnp.abs(a) for a in cosines(dirs, first + dd)]
                    speeds = pace * (ax + ay + az)
                    inv = lazily(lambda j, speeds=speeds: inverse(speeds + rates(j)))

                    def fresh(j, dd=dd, inv=inv):
                        s = sources(j)
                        if at_edge:
                            s = s + seed[dd, hs, cuts[j]]
                        return flow[g * per + dd, x, hs, cuts[j]] + s * inv(j)

                    v = lazily(fresh)
                    shifts = (shift_y(v, n, rising, lane), shift_z(v, n, dd % 2 == 0, lane))
                    ways.append((v, inv, *shifts, (pace * ax, pace * ay, pace * az)))
                for j, cs in enumerate(cuts):
                    kept = []
                    again, level = source1[x, hs, cs], warm[x, :, cs]
                    for dd, (v, inv, along_y, along_z, (cx, cy, cz)) in enumerate(ways):
                        new = inv(j) * add_terms([
                            times(cx, prev[dd, hs, cs]), times(cy, along_y(j)), times(cz, along_z(j)), again
                        ])
                        prev[dd, hs, cs] = v(j)
                        dual[dd, x, hs, cs] = new
                        kept.append((v(j) + new) * (excess[g * per + dd, x, hs, cs] - level))
                    acc[x, hs, cs] += add_terms(kept)

        layer(0, True)

        def later(i, _):
            layer(i, False)
            return 0

        lax.fori_loop(1, nx, later, 0)

    rises = cosines(dirs, first)[1] > 0
    pl.when(rises)(lambda: run(True))
    pl.when(jnp.logical_not(rises))(lambda: run(False))

    @pl.when(g == steps - 1)
    def _():
        for x in range(nx):
            for cs in cuts:
                total = 0.0
                for hs in bands:
                    total = total + base_tile(cols, material[x : x + 1, cs], hs) * acc[x, hs, cs]
                gradient[x : x + 1, cs] = sub_sum(total) * 0.8


def swapped(value, start):
    count = lax.axis_size("space")
    pairs = [(s, s + 1) for s in range(start, count - 1, 2)]
    return lax.ppermute(value, "space", pairs + [(b, a) for a, b in pairs])


def shares(partial):
    size = lax.axis_size("band")
    total = partial
    for k in range(1, size):
        total = total + lax.ppermute(partial, "band", [(s, (s + k) % size) for s in range(size)])
    count = lax.axis_size("dir")
    pairs = count & (count - 1) == 0
    hops = [[(s, s ^ k if pairs else (s + k) % count) for s in range(count)] for k in range(1, count)]
    return [total] + [lax.ppermute(total, "dir", hop) for hop in hops]


def whole(array):
    return pl.BlockSpec(array.shape, lambda *g: (0,) * array.ndim)


def on_device(
    adjoint_start, primal_deviations, density, material, rate_table, group_speed, heat_capacity, objective_weight
):
    count, nb, nx, plane = adjoint_start.shape
    half = count // 2
    first_steps = count // math.gcd(FIRST_GROUP, half)
    second_steps = count // math.gcd(SECOND_GROUP, half)
    nmat = rate_table.shape[0]
    start = adjoint_start.transpose(0, 2, 1, 3)
    excess = primal_deviations.transpose(0, 2, 1, 3)
    f32 = jnp.float32
    vmem = pl.BlockSpec(memory_space=pltpu.VMEM)
    smem = pl.BlockSpec(memory_space=pltpu.SMEM)
    dirs = jnp.asarray(direction_table(count))
    heat = heat_capacity.reshape(1, -1)
    speed = group_speed.reshape(1, -1)
    tables = (heat, speed, rate_table)
    cells = (density, material)
    cols = pltpu.VMEM((2 + nmat, nb, LANES), f32)
    params = pltpu.CompilerParams(vmem_limit_bytes=VMEM_LIMIT)
    size = count * nb * nx * plane

    rows = half * nb + SUB
    hbm = pl.BlockSpec(memory_space=pltpu.HBM)
    small = (rate_table, *cells, objective_weight)
    face_a, face_b = pl.pallas_call(
        faces_kernel,
        out_shape=(jax.ShapeDtypeStruct((rows, plane), f32),) * 2,
        in_specs=[hbm] * 5,
        out_specs=[vmem] * 2,
        scratch_shapes=[pltpu.VMEM(a.shape, a.dtype) for a in small]
        + [pltpu.VMEM((2, half, nb, plane), f32), cols, pltpu.SemaphoreType.DMA((4 + 2 * (half + 1),))],
        compiler_params=params,
        cost_estimate=pl.CostEstimate(flops=size // 3, bytes_accessed=size * 2, transcendentals=0),
        name="faces",
    )(*small, start)
    halo0_a, halo0_b = swapped(face_a, 0), swapped(face_b, 1)

    sum_rows = -(-(4 * nx + 2) // SUB) * SUB
    small = (*tables, *cells)
    flow, face_a, face_b, sums = pl.pallas_call(
        first_kernel,
        grid=(first_steps,),
        out_shape=(
            jax.ShapeDtypeStruct(start.shape, f32),
            jax.ShapeDtypeStruct((half * nb, plane), f32),
            jax.ShapeDtypeStruct((half * nb, plane), f32),
            jax.ShapeDtypeStruct((sum_rows, plane), f32),
        ),
        in_specs=[smem] + [vmem] * (len(small) + 2),
        out_specs=[vmem] * 4,
        scratch_shapes=[cols, pltpu.VMEM((nx, nb, plane), f32), pltpu.VMEM((4, nx, nb, plane), f32)],
        compiler_params=params,
        cost_estimate=pl.CostEstimate(flops=size * 20, bytes_accessed=size * 12, transcendentals=size),
        name="first",
    )(dirs, *small, start, excess)
    halo1_a, halo1_b = swapped(face_a, 0), swapped(face_b, 1)

    sums = pl.pallas_call(
        edges_kernel,
        out_shape=jax.ShapeDtypeStruct(sums.shape, f32),
        in_specs=[smem] + [pl.BlockSpec(memory_space=pltpu.VMEM)] * (len(small) + 3),
        out_specs=pl.BlockSpec(memory_space=pltpu.VMEM),
        scratch_shapes=[cols],
        compiler_params=params,
        cost_estimate=pl.CostEstimate(flops=size, bytes_accessed=size, transcendentals=0),
        name="edges",
    )(dirs, *small, halo0_a, halo0_b, sums)
    parts = shares(sums)
    parts = parts[:3] + [sum(parts[3:], jnp.zeros_like(sums))] if len(parts) > 4 else parts + [jnp.zeros_like(sums)] * (4 - len(parts))

    small = (*tables, *cells, objective_weight, *parts)
    dual, gradient = pl.pallas_call(
        second_kernel,
        grid=(second_steps,),
        out_shape=(jax.ShapeDtypeStruct(start.shape, f32), jax.ShapeDtypeStruct((nx, plane), f32)),
        in_specs=[smem] + [vmem] * (len(small) + 6),
        out_specs=[pl.BlockSpec((count // second_steps, nx, nb, plane), lambda g: (g, 0, 0, 0)), vmem],
        scratch_shapes=[
            cols,
            pltpu.VMEM((nx + 2, nb, plane), f32),
            pltpu.VMEM((nx + 2, nb, plane), f32),
            pltpu.VMEM((nx, nb, plane), f32),
            pltpu.VMEM((nx, SUB, plane), f32),
            pltpu.VMEM((count // second_steps, nb, plane), f32),
            pltpu.VMEM((count // second_steps, nb, plane), f32),
            pltpu.VMEM((nx, nb, plane), f32),
        ],
        compiler_params=params,
        cost_estimate=pl.CostEstimate(flops=size * 30, bytes_accessed=size * 12, transcendentals=size),
        name="second",
    )(dirs, *small, halo0_a, halo0_b, halo1_a, halo1_b, flow, excess)
    gradient = sum(shares(gradient)) * (-0.125 / ITERS)
    return (dual.transpose(0, 2, 1, 3), gradient)


def solution(mesh):
    placed = (
        P("dir", "band", "space", None),
        P("dir", "band", "space", None),
        P("space", None),
        P("space", None),
        P(None, "band"),
        P("band"),
        P(),
        P("space", None),
    )
    return jax.shard_map(
        on_device,
        mesh=mesh,
        in_specs=placed,
        out_specs=(P("dir", "band", "space", None), P("space", None)),
        check_vma=False,
    )
```

```python
import math

import jax
import jax.numpy as jnp
import numpy as np
from jax import lax
from jax.experimental import pallas as pl
from jax.experimental.pallas import tpu as pltpu
from jax.sharding import PartitionSpec as P

NDIR = 64
NB = 32
NY = 192
ITERS = 2
LANES = 128
SUB = 8
FIRST_GROUP = 8
SECOND_GROUP = 4
VMEM_LIMIT = 16 * 1024 * 1024


def direction_table(count):
    d = np.arange(NDIR)
    half = count // 2
    block, slot = d // count, d % count
    side, pair = slot // half, slot % half
    azimuth = np.pi * (block * half + pair + 0.5) / (NDIR // 2) - np.pi / 2
    along_z = 0.4 * (1.0 - 2.0 * (pair % 2))
    tilt = np.sqrt(1.0 - along_z * along_z)
    along_x = (1.0 - 2.0 * side) * tilt * np.cos(azimuth)
    along_y = tilt * np.sin(azimuth)
    return np.stack([along_x, along_y, along_z], axis=1).astype(np.float32).reshape(-1)


def lane_ids():
    return lax.broadcasted_iota(jnp.int32, (SUB, LANES), 1)


def lazily(make):
    made = {}

    def get(j):
        if j not in made:
            made[j] = make(j)
        return made[j]

    return get


def shifted(v, n, offset, lane, masked=None):
    q, rem = divmod(offset, LANES)
    zero = jnp.zeros((SUB, LANES), jnp.float32)
    rolled = lazily(lambda j: pltpu.roll(v(j), LANES - rem, 1) if rem else v(j))

    def tile(j):
        parts = []
        for k, low, high in ((j + q, 0, LANES - rem), (j + q + 1, LANES - rem, LANES)):
            kept = low < high and 0 <= k < n
            kept = kept and not all(masked is not None and masked(j * LANES + i) for i in range(low, high))
            parts.append(rolled(k) if kept else None)
        if parts[0] is None and parts[1] is None:
            return None
        t = parts[0]
        if rem:
            t = jnp.where(lane < LANES - rem, *[zero if part is None else part for part in parts])
        for i in range(LANES):
            if masked is not None and masked(j * LANES + i) and parts[int(i >= LANES - rem)] is not None:
                t = jnp.where(lane == i, zero, t)
        return t

    return lazily(tile)


def shift_y(v, n, rising, lane):
    if rising:
        return shifted(v, n, 1, lane, lambda p: p % NY == NY - 1)
    return shifted(v, n, -1, lane, lambda p: p % NY == 0)


def shift_z(v, n, rising, lane):
    return shifted(v, n, NY if rising else -NY, lane)


def inverse(x):
    r = pl.reciprocal(x, approx=True)
    return r * (2.0 - x * r)


def column(row, offset, n):
    shape = (n, row.shape[1])
    i0 = lax.broadcasted_iota(jnp.int32, shape, 0)
    i1 = lax.broadcasted_iota(jnp.int32, shape, 1)
    picked = jnp.sum(jnp.where(i1 == i0 + offset, row, 0.0), axis=1, keepdims=True)
    return jnp.broadcast_to(picked, (n, LANES))


def fill_columns(cols, heat, speed, table):
    nb = cols.shape[1]
    row = heat[...]
    total = jnp.sum(row, axis=1, keepdims=True) * float(NDIR)
    cols[0] = column(speed[...], 0, nb)
    cols[1] = column(row / total, lax.axis_index("band") * nb, nb)
    for m in range(table.shape[0]):
        cols[2 + m] = column(table[m : m + 1], 0, nb)


def rate_tile(cols, density, material, hs):
    return base_tile(cols, material, hs) * (0.2 + 0.8 * density)


def base_tile(cols, material, hs):
    base = jnp.broadcast_to(cols[2, hs], (SUB, LANES))
    for m in range(1, cols.shape[0] - 2):
        base = jnp.where(material == m, cols[2 + m, hs], base)
    return base


def halves(nb):
    return [slice(h * SUB, (h + 1) * SUB) for h in range(nb // SUB)]


def tiles(plane):
    return [slice(j * LANES, (j + 1) * LANES) for j in range(plane // LANES)]


def sub_sum(t):
    return jnp.sum(t, axis=0, keepdims=True)


def add_terms(terms):
    terms = [t for t in terms if t is not None]
    total = terms[0]
    for t in terms[1:]:
        total = total + t
    return total


def times(a, b):
    return None if b is None else a * b


def cosines(dirs, d):
    at = 3 * d
    return dirs[at], dirs[at + 1], dirs[at + 2]


def is_even():
    return lax.axis_index("space") % 2 == 0


def faces_kernel(
    heat_in, speed_in, table_in, density_in, material_in, objective_in, start,
    out_a, out_b, cols, density, material, objective,
    heat, speed, table, others, sems,
):
    half, nb, plane = others.shape[1:]
    last = density.shape[0] - 1
    even = is_even()
    copies = []
    for n, (src, dst) in enumerate(
        (
            (heat_in, heat), (speed_in, speed), (table_in, table),
            (density_in, density), (material_in, material), (objective_in, objective),
        )
    ):
        copies.append(pltpu.make_async_copy(src, dst, sems.at[n]))
    for side, out in enumerate((out_a, out_b)):
        upper = even if side == 0 else jnp.logical_not(even)
        first, second, x = jnp.where(upper, half, 0), jnp.where(upper, 0, half), jnp.where(upper, last, 0)
        at = 6 + side * (half + 1)
        for d in range(half):
            copies.append(
                pltpu.make_async_copy(start.at[first + d, x], out.at[pl.ds(d * nb, nb)], sems.at[at + d])
            )
        copies.append(pltpu.make_async_copy(start.at[pl.ds(second, half), x], others.at[side], sems.at[at + half]))
    for copy in copies:
        copy.start()
    for copy in copies:
        copy.wait()
    fill_columns(cols, heat, speed, table)
    for side, out in enumerate((out_a, out_b)):
        upper = even if side == 0 else jnp.logical_not(even)
        row = lambda ref, cs: jnp.where(upper, ref[last : last + 1, cs], ref[0:1, cs])
        base = half * nb
        for cs in tiles(plane):
            dens, mat = row(density, cs), row(material, cs)
            share = 0.0
            for h, hs in enumerate(halves(nb)):
                total = others[side, 0, hs, cs]
                for d in range(1, half):
                    total = total + others[side, d, hs, cs]
                for d in range(half):
                    total = total + out[d * nb + h * SUB : d * nb + (h + 1) * SUB, cs]
                share = share + rate_tile(cols, dens, mat, hs) * total
            out[base : base + 1, cs] = sub_sum(share)
            out[base + 1 : base + 2, cs] = dens
            out[base + 2 : base + 3, cs] = mat.astype(jnp.float32)
            out[base + 3 : base + 4, cs] = row(objective, cs)
            out[base + 4 : base + 8, cs] = jnp.zeros((4, LANES), jnp.float32)


def first_kernel(
    dirs, cols, density, material, start, excess_in, flow, excess, face_a, face_b, sums, field, rate, acc, sems
):
    count, nx, nb, plane = field.shape
    half = count // 2
    per = math.gcd(FIRST_GROUP, half)
    groups = count // per
    cuts, bands = tiles(plane), halves(nb)
    n = len(cuts)

    def fetch(x, which):
        src, dst = ((start, field), (excess_in, excess))[which]
        return pltpu.make_async_copy(src.at[:, x], dst.at[:, x], sems.at[which, x])

    for x, which in ((0, 0), (1, 0), (0, 1), (2, 0), (1, 1)):
        if x < nx:
            fetch(x, which).start()
    for x in range(nx):
        for cs in cuts:
            for hs in bands:
                rate[x, hs, cs] = rate_tile(cols, density[x : x + 1, cs], material[x : x + 1, cs], hs)
    acc[...] = jnp.zeros_like(acc)
    block = lax.axis_index("dir")
    lane = lane_ids()
    fetch(0, 0).wait()

    def layer(x, _):
        pl.when(x + 3 < nx)(lambda: fetch(x + 3, 0).start())
        pl.when(x + 2 < nx)(lambda: fetch(x + 2, 1).start())
        pl.when(x + 1 < nx)(lambda: fetch(x + 1, 0).wait())
        fetch(x, 1).wait()

        def group(k, _):
            first = k * per
            ahead = first < half
            edge = jnp.where(ahead, x == nx - 1, x == 0)
            beside = jnp.where(edge, x, jnp.where(ahead, x + 1, x - 1))

            def run(rising):
                for hs in bands:
                    pace = cols[0, hs]
                    ways = []
                    for dd in range(per):
                        ax, ay, az = [jnp.abs(a) for a in cosines(dirs, block * count + first + dd)]
                        v = lazily(lambda j, dd=dd: field[first + dd, x, hs, cuts[j]])
                        speeds = (pace * jnp.where(edge, 0.0, ax), pace * ay, pace * az, pace * (ax + ay + az))
                        ways.append((v, shift_y(v, n, rising, lane), shift_z(v, n, dd % 2 == 0, lane), speeds))
                    for j, cs in enumerate(cuts):
                        r = rate[x, hs, cs]
                        kept = []
                        for dd, (v, along_y, along_z, (cx, cy, cz, speeds)) in enumerate(ways):
                            d = first + dd
                            inv = inverse(speeds + r)
                            a = inv * add_terms(
                                [times(cx, field[d, beside, hs, cs]), times(cy, along_y(j)), times(cz, along_z(j))]
                            )
                            flow[d, x, hs, cs] = a
                            kept.append((v(j), excess[d, x, hs, cs], a, inv))
                        for f in range(4):
                            acc[f, x, hs, cs] += add_terms([k[f] for k in kept])

            rises = cosines(dirs, block * count + first)[1] > 0
            pl.when(rises)(lambda: run(True))
            pl.when(jnp.logical_not(rises))(lambda: run(False))
            return 0

        lax.fori_loop(0, groups, group, 0)
        return 0

    lax.fori_loop(0, nx, layer, 0)
    even = is_even()
    for face, upper in ((face_a, even), (face_b, jnp.logical_not(even))):
        first, x = jnp.where(upper, half, 0), jnp.where(upper, nx - 1, 0)
        for d in range(half):
            face[d * nb : (d + 1) * nb] = flow[first + d, x]
    for x in range(nx):
        for cs in cuts:
            totals = [0.0] * 4
            for hs in bands:
                r, w = rate[x, hs, cs], cols[1, hs]
                for f, scale in enumerate((r, w, r, r * w)):
                    totals[f] = totals[f] + scale * acc[f, x, hs, cs]
            for f in range(4):
                sums[f * nx + x : f * nx + x + 1, cs] = sub_sum(totals[f])
    sums[4 * nx :] = jnp.zeros((sums.shape[0] - 4 * nx, plane), jnp.float32)


def edges_kernel(dirs, cols, density, material, halo_a, halo_b, sums, out):
    nx, plane = density.shape
    nb = cols.shape[1]
    half = (halo_a.shape[0] - SUB) // nb
    count = 2 * half
    block = lax.axis_index("dir")
    even = is_even()
    out[...] = sums[...]
    cuts = tiles(plane)
    gains = []
    for side, halo in enumerate((halo_a, halo_b)):
        ahead = even if side == 0 else jnp.logical_not(even)
        rates = []
        for hs in halves(nb):
            rates.append([])
            for cs in cuts:
                mat = jnp.where(ahead, material[nx - 1 : nx, cs], material[0:1, cs])
                dens = jnp.where(ahead, density[nx - 1 : nx, cs], density[0:1, cs])
                rates[-1].append(rate_tile(cols, dens, mat, hs))
        first = block * count + jnp.where(ahead, 0, half)

        def add(d, totals):
            ax, ay, az = [jnp.abs(a) for a in cosines(dirs, first + d)]
            new = list(totals)
            for h, hs in enumerate(halves(nb)):
                pace = cols[0, hs]
                cx, speeds = pace * ax, pace * (ax + ay + az)
                rows = halo.at[pl.ds(pl.multiple_of(d * nb + h * SUB, SUB), SUB)]
                for j, cs in enumerate(cuts):
                    r = rates[h][j]
                    new[j] = new[j] + (cx * rows[:, cs]) * (r * inverse(speeds + r))
            return tuple(new)

        totals = lax.fori_loop(0, half, add, tuple(jnp.zeros((SUB, LANES), jnp.float32) for _ in cuts))
        gains.append([sub_sum(t) for t in totals])
    base = half * nb
    for side, x in enumerate((nx - 1, 0)):
        near, far = (0, 1) if side == 0 else (1, 0)
        row = 2 * nx + x
        for j, cs in enumerate(cuts):
            out[row : row + 1, cs] = out[row : row + 1, cs] + jnp.where(even, gains[near][j], gains[far][j])
            a, b = halo_a[base : base + 1, cs], halo_b[base : base + 1, cs]
            out[4 * nx + side : 4 * nx + side + 1, cs] = jnp.where(even, a, b) if side == 0 else jnp.where(even, b, a)


def second_kernel(
    dirs, cols, density, material, objective, sum0, sum1, sum2, sum3, halo0_a, halo0_b, flow, excess,
    dual, edge_dual, known, gradient,
    rate, source0, source1, warm, prev, seed, acc,
):
    g = pl.program_id(0)
    steps = pl.num_programs(0)
    count, nx, nb, plane = flow.shape
    per = count // steps
    cuts, bands = tiles(plane), halves(nb)
    n = len(cuts)
    scale = float(NDIR * NB)
    edge = halo0_a.shape[0] - SUB

    @pl.when(g == 0)
    def _():
        total = (sum0[...] + sum1[...]) + (sum2[...] + sum3[...])
        for x in range(nx):
            warm[x] = jnp.broadcast_to(total[nx + x : nx + x + 1], (SUB, plane))
        known[0:1] = total[2 * nx - 1 : 2 * nx]
        known[1:2] = total[nx : nx + 1]
        for side in range(2):
            from_a = is_even() if side == 0 else jnp.logical_not(is_even())
            aim = jnp.where(from_a, halo0_a[edge + 3 : edge + 4], halo0_b[edge + 3 : edge + 4])
            known[2 + side : 3 + side] = total[4 * nx + side : 4 * nx + side + 1] + scale * aim
        known[4:8] = jnp.zeros((4, plane), jnp.float32)
        for x in range(nx):
            for cs in cuts:
                drive = total[x : x + 1, cs] + scale * objective[x : x + 1, cs]
                again = (
                    total[2 * nx + x : 2 * nx + x + 1, cs]
                    + drive * total[3 * nx + x : 3 * nx + x + 1, cs]
                    + scale * objective[x : x + 1, cs]
                )
                for hs in bands:
                    w = cols[1, hs]
                    rate[x, hs, cs] = rate_tile(cols, density[x : x + 1, cs], material[x : x + 1, cs], hs)
                    source0[x, hs, cs] = w * drive
                    source1[x, hs, cs] = w * again
        acc[...] = jnp.zeros_like(acc)

    block = lax.axis_index("dir")
    first = block * count + g * per
    ahead = g < steps // 2
    lane = lane_ids()

    def enter(halo0):
        skip = jnp.where(ahead, 0, steps // 2)
        for dd in range(per):
            ax = jnp.abs(cosines(dirs, first + dd)[0])
            for h, hs in enumerate(bands):
                cx = cols[0, hs] * ax
                rows = pl.ds(pl.multiple_of(((g - skip) * per + dd) * nb + h * SUB, SUB), SUB)
                for cs in cuts:
                    seed[dd, hs, cs] = cx * halo0[rows, cs]

    pl.when(ahead == is_even())(lambda: enter(halo0_a))
    pl.when(ahead != is_even())(lambda: enter(halo0_b))

    def run(rising):
        def layer(i, at_edge):
            x = jnp.where(ahead, nx - 1 - i, i)
            for hs in bands:
                pace = cols[0, hs]
                rates = lazily(lambda j: rate[x, hs, cuts[j]])
                sources = lazily(lambda j: source0[x, hs, cuts[j]])
                ways = []
                for dd in range(per):
                    ax, ay, az = [jnp.abs(a) for a in cosines(dirs, first + dd)]
                    speeds = pace * (ax + ay + az)
                    inv = lazily(lambda j, speeds=speeds: inverse(speeds + rates(j)))

                    def fresh(j, dd=dd, inv=inv):
                        s = sources(j)
                        if at_edge:
                            s = s + seed[dd, hs, cuts[j]]
                        return flow[g * per + dd, x, hs, cuts[j]] + s * inv(j)

                    v = lazily(fresh)
                    shifts = (shift_y(v, n, rising, lane), shift_z(v, n, dd % 2 == 0, lane))
                    ways.append((v, inv, *shifts, (pace * ax, pace * ay, pace * az)))
                for j, cs in enumerate(cuts):
                    kept = []
                    again, level = source1[x, hs, cs], warm[x, :, cs]
                    for dd, (v, inv, along_y, along_z, (cx, cy, cz)) in enumerate(ways):
                        beside = None if at_edge else cx * prev[dd, hs, cs]
                        new = inv(j) * add_terms([beside, times(cy, along_y(j)), times(cz, along_z(j)), again])
                        prev[dd, hs, cs] = v(j)
                        dual[dd, x, hs, cs] = new
                        if at_edge:
                            edge_dual[g * per + dd, hs, cs] = new
                        kept.append((v(j) + new) * (excess[g * per + dd, x, hs, cs] - level))
                    acc[x, hs, cs] += add_terms(kept)

        layer(0, True)

        def later(i, _):
            layer(i, False)
            return 0

        lax.fori_loop(1, nx, later, 0)

    rises = cosines(dirs, first)[1] > 0
    pl.when(rises)(lambda: run(True))
    pl.when(jnp.logical_not(rises))(lambda: run(False))

    @pl.when(g == steps - 1)
    def _():
        for x in range(nx):
            for cs in cuts:
                total = 0.0
                for hs in bands:
                    total = total + base_tile(cols, material[x : x + 1, cs], hs) * acc[x, hs, cs]
                gradient[x : x + 1, cs] = sub_sum(total) * 0.8


def last_kernel(
    dirs, cols, density, material, halo0_a, halo0_b, halo1_a, halo1_b, excess, edge_dual, known, gradient, dual_in,
    dual, out, done, sems,
):
    nx, plane = density.shape
    count, nb = edge_dual.shape[:2]
    half = count // 2
    cuts, bands = tiles(plane), halves(nb)
    params = halo0_a.shape[0] - SUB
    block = lax.axis_index("dir")
    even = is_even()
    copies = []
    gains = []
    for part, (halo0, halo1) in enumerate(((halo0_a, halo1_a), (halo0_b, halo1_b))):
        ahead = even if part == 0 else jnp.logical_not(even)
        first, x = jnp.where(ahead, 0, half), jnp.where(ahead, nx - 1, 0)

        def pick(ref, i, k, cs):
            return jnp.where(ahead, ref[i : i + 1, cs], ref[k : k + 1, cs])

        sums = []
        for cs in cuts:
            dens, mat = pick(density, nx - 1, 0, cs), pick(material, nx - 1, 0, cs)
            beyond = halo0[params + 1 : params + 2, cs]
            beyond_mat = halo0[params + 2 : params + 3, cs].astype(jnp.int32)
            level, drive = pick(known, 0, 1, cs), pick(known, 2, 3, cs)
            share = 0.0
            for h, hs in enumerate(bands):
                pace, base = cols[0, hs], base_tile(cols, mat, hs)
                r, r_beyond = base * (0.2 + 0.8 * dens), rate_tile(cols, beyond, beyond_mat, hs)
                source = cols[1, hs] * drive

                def add(d, total):
                    ax, ay, az = [jnp.abs(a) for a in cosines(dirs, block * count + first + d)]
                    speeds, cx = pace * (ax + ay + az), pace * ax
                    rows = pl.ds(pl.multiple_of(d * nb + h * SUB, SUB), SUB)
                    v = halo1[rows, cs] + source * inverse(speeds + r_beyond)
                    new = (cx * v) * inverse(speeds + r)
                    done[first + d, hs, cs] = edge_dual[first + d, hs, cs] + new
                    return total + new * (excess[first + d, x, hs, cs] - level)

                total = lax.fori_loop(0, half, add, jnp.zeros((SUB, LANES), jnp.float32), unroll=True)
                share = share + base * total
            sums.append(sub_sum(share) * 0.8)
        gains.append(sums)
        copy = pltpu.make_async_copy(done.at[pl.ds(first, half)], dual.at[pl.ds(first, half), x], sems.at[part])
        copy.start()
        copies.append(copy)
    out[...] = gradient[...]
    for j, cs in enumerate(cuts):
        out[nx - 1 : nx, cs] = out[nx - 1 : nx, cs] + jnp.where(even, gains[0][j], gains[1][j])
        out[0:1, cs] = out[0:1, cs] + jnp.where(even, gains[1][j], gains[0][j])
    for copy in copies:
        copy.wait()


def swapped(value, start):
    count = lax.axis_size("space")
    pairs = [(s, s + 1) for s in range(start, count - 1, 2)]
    return lax.ppermute(value, "space", pairs + [(b, a) for a, b in pairs])


def shares(partial):
    size = lax.axis_size("band")
    total = partial
    for k in range(1, size):
        total = total + lax.ppermute(partial, "band", [(s, (s + k) % size) for s in range(size)])
    count = lax.axis_size("dir")
    pairs = count & (count - 1) == 0
    hops = [[(s, s ^ k if pairs else (s + k) % count) for s in range(count)] for k in range(1, count)]
    return [total] + [lax.ppermute(total, "dir", hop) for hop in hops]


def whole(array):
    return pl.BlockSpec(array.shape, lambda *g: (0,) * array.ndim)


def on_device(
    adjoint_start, primal_deviations, density, material, rate_table, group_speed, heat_capacity, objective_weight
):
    count, nb, nx, plane = adjoint_start.shape
    half = count // 2
    first_steps = count // math.gcd(FIRST_GROUP, half)
    second_steps = count // math.gcd(SECOND_GROUP, half)
    nmat = rate_table.shape[0]
    start = adjoint_start.transpose(0, 2, 1, 3)
    excess = primal_deviations.transpose(0, 2, 1, 3)
    f32 = jnp.float32
    vmem = pl.BlockSpec(memory_space=pltpu.VMEM)
    smem = pl.BlockSpec(memory_space=pltpu.SMEM)
    vmem = pl.BlockSpec(memory_space=pltpu.VMEM)
    hbm = pl.BlockSpec(memory_space=pltpu.HBM)
    dirs = jnp.asarray(direction_table(count))
    params = pltpu.CompilerParams(vmem_limit_bytes=VMEM_LIMIT)
    size = count * nb * nx * plane

    def stay(*arrays):
        return [pltpu.with_memory_space_constraint(a, pltpu.HBM) for a in arrays]

    def like(*shape):
        return jax.ShapeDtypeStruct(shape, f32)

    def cost(work, moved):
        return pl.CostEstimate(flops=int(size * work), bytes_accessed=int(size * moved), transcendentals=0)

    small = (heat_capacity.reshape(1, -1), group_speed.reshape(1, -1), rate_table)
    cells = (density, material, objective_weight)
    face_a, face_b, cols, density, material, objective = pl.pallas_call(
        faces_kernel,
        out_shape=(
            like(half * nb + SUB, plane), like(half * nb + SUB, plane), like(2 + nmat, nb, LANES),
            *(jax.ShapeDtypeStruct(a.shape, a.dtype) for a in cells),
        ),
        in_specs=[hbm] * 7,
        out_specs=[vmem] * 6,
        scratch_shapes=[pltpu.VMEM(a.shape, a.dtype) for a in small]
        + [pltpu.VMEM((2, half, nb, plane), f32), pltpu.SemaphoreType.DMA((6 + 2 * (half + 1),))],
        compiler_params=params,
        cost_estimate=cost(0.3, 2),
        name="faces",
    )(*stay(*small, *cells, start))
    halo0_a, halo0_b = swapped(face_a, 0), swapped(face_b, 1)

    sum_rows = -(-(4 * nx + 2) // SUB) * SUB
    flow, excess, face_a, face_b, sums = pl.pallas_call(
        first_kernel,
        out_shape=(
            like(*start.shape), like(*start.shape), like(half * nb, plane), like(half * nb, plane), like(sum_rows, plane)
        ),
        in_specs=[smem] + [vmem] * 3 + [hbm] * 2,
        out_specs=[vmem] * 5,
        scratch_shapes=[
            pltpu.VMEM(start.shape, f32), pltpu.VMEM((nx, nb, plane), f32), pltpu.VMEM((4, nx, nb, plane), f32),
            pltpu.SemaphoreType.DMA((2, nx)),
        ],
        compiler_params=params,
        cost_estimate=cost(20, 12),
        name="first",
    )(dirs, cols, density, material, *stay(start, excess))
    halo1_a, halo1_b = swapped(face_a, 0), swapped(face_b, 1)

    sums = pl.pallas_call(
        edges_kernel,
        out_shape=like(sum_rows, plane),
        in_specs=[smem] + [vmem] * 6,
        out_specs=vmem,
        compiler_params=params,
        cost_estimate=cost(1, 1),
        name="edges",
    )(dirs, cols, density, material, halo0_a, halo0_b, sums)
    parts = shares(sums)
    parts = parts + [jnp.zeros_like(sums)] * (4 - len(parts))
    parts = parts[:3] + [sum(parts[4:], parts[3])]

    second_steps = count // math.gcd(SECOND_GROUP, half)
    per = count // second_steps
    layer = pltpu.VMEM((nx, nb, plane), f32)
    dual, edge_dual, known, gradient = pl.pallas_call(
        second_kernel,
        grid=(second_steps,),
        out_shape=(like(*start.shape), like(count, nb, plane), like(SUB, plane), like(nx, plane)),
        in_specs=[smem] + [vmem] * 12,
        out_specs=[pl.BlockSpec((per, nx, nb, plane), lambda g: (g, 0, 0, 0))] + [vmem] * 3,
        scratch_shapes=[
            layer, layer, layer, pltpu.VMEM((nx, SUB, plane), f32),
            pltpu.VMEM((per, nb, plane), f32), pltpu.VMEM((per, nb, plane), f32), layer,
        ],
        compiler_params=params,
        cost_estimate=cost(30, 12),
        name="second",
    )(dirs, cols, density, material, objective, *parts, halo0_a, halo0_b, flow, excess)

    dual, gradient = pl.pallas_call(
        last_kernel,
        out_shape=(like(*start.shape), like(nx, plane)),
        in_specs=[smem] + [vmem] * 11 + [hbm],
        out_specs=[hbm, vmem],
        scratch_shapes=[pltpu.VMEM((count, nb, plane), f32), pltpu.SemaphoreType.DMA((2,))],
        input_output_aliases={12: 0},
        compiler_params=params,
        cost_estimate=cost(1, 1),
        name="last",
    )(dirs, cols, density, material, halo0_a, halo0_b, halo1_a, halo1_b, excess, edge_dual, known, gradient, dual)
    gradient = sum(shares(gradient)) * (-0.125 / ITERS)
    return (dual.transpose(0, 2, 1, 3), gradient)


def solution(mesh):
    placed = (
        P("dir", "band", "space", None),
        P("dir", "band", "space", None),
        P("space", None),
        P("space", None),
        P(None, "band"),
        P("band"),
        P(),
        P("space", None),
    )
    return jax.shard_map(
        on_device,
        mesh=mesh,
        in_specs=placed,
        out_specs=(P("dir", "band", "space", None), P("space", None)),
        check_vma=False,
    )
```

```python
import math

import jax
import jax.numpy as jnp
import numpy as np
from jax import lax
from jax.experimental import pallas as pl
from jax.experimental.pallas import tpu as pltpu
from jax.sharding import PartitionSpec as P

NDIR = 64
NB = 32
NY = 192
ITERS = 2
LANES = 128
SUB = 8
FIRST_GROUP = 8
SECOND_GROUP = 8
SLOTS = 5
VMEM_LIMIT = 18 * 1024 * 1024


def direction_table(count):
    d = np.arange(NDIR)
    half = count // 2
    block, slot = d // count, d % count
    side, pair = slot // half, slot % half
    azimuth = np.pi * (block * half + pair + 0.5) / (NDIR // 2) - np.pi / 2
    along_z = 0.4 * (1.0 - 2.0 * (pair % 2))
    tilt = np.sqrt(1.0 - along_z * along_z)
    along_x = (1.0 - 2.0 * side) * tilt * np.cos(azimuth)
    along_y = tilt * np.sin(azimuth)
    return np.stack([along_x, along_y, along_z], axis=1).astype(np.float32).reshape(-1)


def lane_ids():
    return lax.broadcasted_iota(jnp.int32, (SUB, LANES), 1)


def lazily(make):
    made = {}

    def get(j):
        if j not in made:
            made[j] = make(j)
        return made[j]

    return get


def shifted(v, n, offset, lane, masked=None):
    q, rem = divmod(offset, LANES)
    zero = jnp.zeros((SUB, LANES), jnp.float32)
    rolled = lazily(lambda j: pltpu.roll(v(j), LANES - rem, 1) if rem else v(j))

    def tile(j):
        parts = []
        for k, low, high in ((j + q, 0, LANES - rem), (j + q + 1, LANES - rem, LANES)):
            kept = low < high and 0 <= k < n
            kept = kept and not all(masked is not None and masked(j * LANES + i) for i in range(low, high))
            parts.append(rolled(k) if kept else None)
        if parts[0] is None and parts[1] is None:
            return None
        t = parts[0]
        if rem:
            t = jnp.where(lane < LANES - rem, *[zero if part is None else part for part in parts])
        for i in range(LANES):
            if masked is not None and masked(j * LANES + i) and parts[int(i >= LANES - rem)] is not None:
                t = jnp.where(lane == i, zero, t)
        return t

    return lazily(tile)


def shift_y(v, n, rising, lane):
    if rising:
        return shifted(v, n, 1, lane, lambda p: p % NY == NY - 1)
    return shifted(v, n, -1, lane, lambda p: p % NY == 0)


def shift_z(v, n, rising, lane):
    return shifted(v, n, NY if rising else -NY, lane)


def inverse(x):
    r = pl.reciprocal(x, approx=True)
    return r * (2.0 - x * r)


def column(row, offset, n):
    shape = (n, row.shape[1])
    i0 = lax.broadcasted_iota(jnp.int32, shape, 0)
    i1 = lax.broadcasted_iota(jnp.int32, shape, 1)
    picked = jnp.sum(jnp.where(i1 == i0 + offset, row, 0.0), axis=1, keepdims=True)
    return jnp.broadcast_to(picked, (n, LANES))


def fill_columns(cols, heat, speed, table):
    nb = cols.shape[1]
    row = heat[...]
    total = jnp.sum(row, axis=1, keepdims=True) * float(NDIR)
    cols[0] = column(speed[...], 0, nb)
    cols[1] = column(row / total, lax.axis_index("band") * nb, nb)
    for m in range(table.shape[0]):
        cols[2 + m] = column(table[m : m + 1], 0, nb)


def rate_tile(cols, density, material, hs):
    return base_tile(cols, material, hs) * (0.2 + 0.8 * density)


def base_tile(cols, material, hs):
    base = jnp.broadcast_to(cols[2, hs], (SUB, LANES))
    for m in range(1, cols.shape[0] - 2):
        base = jnp.where(material == m, cols[2 + m, hs], base)
    return base


def halves(nb):
    return [slice(h * SUB, (h + 1) * SUB) for h in range(nb // SUB)]


def tiles(plane):
    return [slice(j * LANES, (j + 1) * LANES) for j in range(plane // LANES)]


def sub_sum(t):
    return jnp.sum(t, axis=0, keepdims=True)


def add_terms(terms):
    terms = [t for t in terms if t is not None]
    total = terms[0]
    for t in terms[1:]:
        total = total + t
    return total


def times(a, b):
    return None if b is None else a * b


def cosines(dirs, d):
    at = 3 * d
    return dirs[at], dirs[at + 1], dirs[at + 2]


def is_even():
    return lax.axis_index("space") % 2 == 0


def faces_kernel(
    heat_in, speed_in, table_in, density_in, material_in, objective_in, start,
    out_a, out_b, cols, density, material, objective,
    heat, speed, table, others, sems,
):
    half, nb, plane = others.shape[1:]
    last = density.shape[0] - 1
    even = is_even()
    copies = []
    for n, (src, dst) in enumerate(
        (
            (heat_in, heat), (speed_in, speed), (table_in, table),
            (density_in, density), (material_in, material), (objective_in, objective),
        )
    ):
        copies.append(pltpu.make_async_copy(src, dst, sems.at[n]))
    for side, out in enumerate((out_a, out_b)):
        upper = even if side == 0 else jnp.logical_not(even)
        first, second, x = jnp.where(upper, half, 0), jnp.where(upper, 0, half), jnp.where(upper, last, 0)
        at = 6 + side * (half + 1)
        for d in range(half):
            copies.append(
                pltpu.make_async_copy(start.at[first + d, x], out.at[pl.ds(d * nb, nb)], sems.at[at + d])
            )
        copies.append(pltpu.make_async_copy(start.at[pl.ds(second, half), x], others.at[side], sems.at[at + half]))
    for copy in copies:
        copy.start()
    for copy in copies:
        copy.wait()
    fill_columns(cols, heat, speed, table)
    for side, out in enumerate((out_a, out_b)):
        upper = even if side == 0 else jnp.logical_not(even)
        row = lambda ref, cs: jnp.where(upper, ref[last : last + 1, cs], ref[0:1, cs])
        base = half * nb
        for cs in tiles(plane):
            dens, mat = row(density, cs), row(material, cs)
            share = 0.0
            for h, hs in enumerate(halves(nb)):
                total = others[side, 0, hs, cs]
                for d in range(1, half):
                    total = total + others[side, d, hs, cs]
                for d in range(half):
                    total = total + out[d * nb + h * SUB : d * nb + (h + 1) * SUB, cs]
                share = share + rate_tile(cols, dens, mat, hs) * total
            out[base : base + 1, cs] = sub_sum(share)
            out[base + 1 : base + 2, cs] = dens
            out[base + 2 : base + 3, cs] = mat.astype(jnp.float32)
            out[base + 3 : base + 4, cs] = row(objective, cs)
            out[base + 4 : base + 8, cs] = jnp.zeros((4, LANES), jnp.float32)


def first_kernel(
    dirs, cols, density, material, start, excess_in, flow, excess, face_a, face_b, sums, field, rate, acc, sems
):
    count, nx, nb, plane = field.shape
    half = count // 2
    per = math.gcd(FIRST_GROUP, half)
    groups = count // per
    cuts, bands = tiles(plane), halves(nb)
    n = len(cuts)

    def fetch(x, which):
        src, dst = ((start, field), (excess_in, excess))[which]
        return pltpu.make_async_copy(src.at[:, x], dst.at[:, x], sems.at[which, x])

    for x, which in ((0, 0), (1, 0), (0, 1), (2, 0), (1, 1)):
        if x < nx:
            fetch(x, which).start()
    for x in range(nx):
        for cs in cuts:
            for hs in bands:
                rate[x, hs, cs] = rate_tile(cols, density[x : x + 1, cs], material[x : x + 1, cs], hs)
    acc[...] = jnp.zeros_like(acc)
    block = lax.axis_index("dir")
    lane = lane_ids()
    fetch(0, 0).wait()

    def layer(x, _):
        pl.when(x + 3 < nx)(lambda: fetch(x + 3, 0).start())
        pl.when(x + 2 < nx)(lambda: fetch(x + 2, 1).start())
        pl.when(x + 1 < nx)(lambda: fetch(x + 1, 0).wait())
        fetch(x, 1).wait()

        def group(k, _):
            first = k * per
            ahead = first < half
            edge = jnp.where(ahead, x == nx - 1, x == 0)
            beside = jnp.where(edge, x, jnp.where(ahead, x + 1, x - 1))

            def run(rising):
                for hs in bands:
                    pace = cols[0, hs]
                    ways = []
                    for dd in range(per):
                        ax, ay, az = [jnp.abs(a) for a in cosines(dirs, block * count + first + dd)]
                        v = lazily(lambda j, dd=dd: field[first + dd, x, hs, cuts[j]])
                        speeds = (pace * jnp.where(edge, 0.0, ax), pace * ay, pace * az, pace * (ax + ay + az))
                        ways.append((v, shift_y(v, n, rising, lane), shift_z(v, n, dd % 2 == 0, lane), speeds))
                    for j, cs in enumerate(cuts):
                        r = rate[x, hs, cs]
                        kept = []
                        for dd, (v, along_y, along_z, (cx, cy, cz, speeds)) in enumerate(ways):
                            d = first + dd
                            inv = inverse(speeds + r)
                            a = inv * add_terms(
                                [times(cx, field[d, beside, hs, cs]), times(cy, along_y(j)), times(cz, along_z(j))]
                            )
                            flow[d, x, hs, cs] = a
                            kept.append((v(j), excess[d, x, hs, cs], a, inv))
                        for f in range(4):
                            acc[f, x, hs, cs] += add_terms([k[f] for k in kept])

            rises = cosines(dirs, block * count + first)[1] > 0
            pl.when(rises)(lambda: run(True))
            pl.when(jnp.logical_not(rises))(lambda: run(False))
            return 0

        lax.fori_loop(0, groups, group, 0)
        return 0

    lax.fori_loop(0, nx, layer, 0)
    even = is_even()
    for face, upper in ((face_a, even), (face_b, jnp.logical_not(even))):
        first, x = jnp.where(upper, half, 0), jnp.where(upper, nx - 1, 0)
        for d in range(half):
            face[d * nb : (d + 1) * nb] = flow[first + d, x]
    for x in range(nx):
        for cs in cuts:
            totals = [0.0] * 4
            for hs in bands:
                r, w = rate[x, hs, cs], cols[1, hs]
                for f, scale in enumerate((r, w, r, r * w)):
                    totals[f] = totals[f] + scale * acc[f, x, hs, cs]
            for f in range(4):
                sums[f * nx + x : f * nx + x + 1, cs] = sub_sum(totals[f])


def edges_kernel(dirs, cols, density, material, halo_a, halo_b, out):
    nx, plane = density.shape
    nb = cols.shape[1]
    half = (halo_a.shape[0] - SUB) // nb
    count = 2 * half
    block = lax.axis_index("dir")
    even = is_even()
    cuts = tiles(plane)
    gains = []
    for side, halo in enumerate((halo_a, halo_b)):
        ahead = even if side == 0 else jnp.logical_not(even)
        rates = []
        for hs in halves(nb):
            rates.append([])
            for cs in cuts:
                mat = jnp.where(ahead, material[nx - 1 : nx, cs], material[0:1, cs])
                dens = jnp.where(ahead, density[nx - 1 : nx, cs], density[0:1, cs])
                rates[-1].append(rate_tile(cols, dens, mat, hs))
        first = block * count + jnp.where(ahead, 0, half)

        def add(d, totals):
            ax, ay, az = [jnp.abs(a) for a in cosines(dirs, first + d)]
            new = list(totals)
            for h, hs in enumerate(halves(nb)):
                pace = cols[0, hs]
                cx, speeds = pace * ax, pace * (ax + ay + az)
                rows = halo.at[pl.ds(pl.multiple_of(d * nb + h * SUB, SUB), SUB)]
                for j, cs in enumerate(cuts):
                    r = rates[h][j]
                    new[j] = new[j] + (cx * rows[:, cs]) * (r * inverse(speeds + r))
            return tuple(new)

        totals = lax.fori_loop(0, half, add, tuple(jnp.zeros((SUB, LANES), jnp.float32) for _ in cuts))
        gains.append([sub_sum(t) for t in totals])
    base = half * nb
    for side in range(2):
        near, far = (0, 1) if side == 0 else (1, 0)
        for j, cs in enumerate(cuts):
            out[side : side + 1, cs] = jnp.where(even, gains[near][j], gains[far][j])
            a, b = halo_a[base : base + 1, cs], halo_b[base : base + 1, cs]
            out[2 + side : 3 + side, cs] = jnp.where(even, a, b) if side == 0 else jnp.where(even, b, a)
    out[4:] = jnp.zeros((out.shape[0] - 4, plane), jnp.float32)


def second_kernel(
    dirs, cols, density, material, objective, sum0, sum1, sum2, sum3, add0, add1, add2, add3, halo0_a, halo0_b, flow, excess,
    dual, edge_dual, known, gradient,
    rate, source0, source1, warm, prev, seed, acc, stage, sems,
):
    count, nx, nb, plane = flow.shape
    half = count // 2
    per = prev.shape[0]
    slots = stage.shape[0]
    cuts, bands = tiles(plane), halves(nb)
    n = len(cuts)
    scale = float(NDIR * NB)
    edge = halo0_a.shape[0] - SUB
    even = is_even()

    total = (sum0[...] + sum1[...]) + (sum2[...] + sum3[...])
    more = (add0[...] + add1[...]) + (add2[...] + add3[...])
    for x in range(nx):
        warm[x] = jnp.broadcast_to(total[nx + x : nx + x + 1], (SUB, plane))
    known[0:1] = total[2 * nx - 1 : 2 * nx]
    known[1:2] = total[nx : nx + 1]
    for side in range(2):
        from_a = even if side == 0 else jnp.logical_not(even)
        aim = jnp.where(from_a, halo0_a[edge + 3 : edge + 4], halo0_b[edge + 3 : edge + 4])
        known[2 + side : 3 + side] = more[2 + side : 3 + side] + scale * aim
    known[4:8] = jnp.zeros((4, plane), jnp.float32)
    for x in range(nx):
        for cs in cuts:
            drive = total[x : x + 1, cs] + scale * objective[x : x + 1, cs]
            again = (
                total[2 * nx + x : 2 * nx + x + 1, cs]
                + drive * total[3 * nx + x : 3 * nx + x + 1, cs]
                + scale * objective[x : x + 1, cs]
            )
            if x == nx - 1:
                again = again + more[0:1, cs]
            if x == 0:
                again = again + more[1:2, cs]
            for hs in bands:
                w = cols[1, hs]
                rate[x, hs, cs] = rate_tile(cols, density[x : x + 1, cs], material[x : x + 1, cs], hs)
                source0[x, hs, cs] = w * drive
                source1[x, hs, cs] = w * again
    acc[...] = jnp.zeros_like(acc)
    block = lax.axis_index("dir")
    lane = lane_ids()

    def sent(first, x, slot):
        return pltpu.make_async_copy(stage.at[slot], dual.at[pl.ds(first, per), x], sems.at[slot])

    def group(k, _):
        first = k * per
        ahead = first < half

        def enter(halo0):
            skip = jnp.where(ahead, 0, half)
            for dd in range(per):
                ax = jnp.abs(cosines(dirs, block * count + first + dd)[0])
                for h, hs in enumerate(bands):
                    cx = cols[0, hs] * ax
                    rows = pl.ds(pl.multiple_of((first - skip + dd) * nb + h * SUB, SUB), SUB)
                    for cs in cuts:
                        seed[dd, hs, cs] = cx * halo0[rows, cs]

        pl.when(ahead == even)(lambda: enter(halo0_a))
        pl.when(ahead != even)(lambda: enter(halo0_b))

        def run(rising):
            def layer(i, at_edge):
                x = jnp.where(ahead, nx - 1 - i, i)
                turn = k * (nx - 1) + i - 1
                slot = turn % slots
                if not at_edge:
                    pl.when(turn >= slots)(lambda: sent(first, x, slot).wait())
                for hs in bands:
                    pace = cols[0, hs]
                    rates = lazily(lambda j: rate[x, hs, cuts[j]])
                    sources = lazily(lambda j: source0[x, hs, cuts[j]])
                    ways = []
                    for dd in range(per):
                        ax, ay, az = [jnp.abs(a) for a in cosines(dirs, block * count + first + dd)]
                        speeds = pace * (ax + ay + az)
                        inv = lazily(lambda j, speeds=speeds: inverse(speeds + rates(j)))

                        def fresh(j, dd=dd, inv=inv):
                            s = sources(j)
                            if at_edge:
                                s = s + seed[dd, hs, cuts[j]]
                            return flow[first + dd, x, hs, cuts[j]] + s * inv(j)

                        v = lazily(fresh)
                        shifts = (shift_y(v, n, rising, lane), shift_z(v, n, dd % 2 == 0, lane))
                        ways.append((v, inv, *shifts, (pace * ax, pace * ay, pace * az)))
                    for j, cs in enumerate(cuts):
                        kept = []
                        again, level = source1[x, hs, cs], warm[x, :, cs]
                        for dd, (v, inv, along_y, along_z, (cx, cy, cz)) in enumerate(ways):
                            beside = None if at_edge else cx * prev[dd, hs, cs]
                            new = inv(j) * add_terms([beside, times(cy, along_y(j)), times(cz, along_z(j)), again])
                            prev[dd, hs, cs] = v(j)
                            if at_edge:
                                edge_dual[first + dd, hs, cs] = new
                            else:
                                stage[slot, dd, hs, cs] = new
                            kept.append((v(j) + new) * (excess[first + dd, x, hs, cs] - level))
                        acc[x, hs, cs] += add_terms(kept)
                if not at_edge:
                    sent(first, x, slot).start()

            layer(0, True)

            def later(i, _):
                layer(i, False)
                return 0

            lax.fori_loop(1, nx, later, 0)

        rises = cosines(dirs, block * count + first)[1] > 0
        pl.when(rises)(lambda: run(True))
        pl.when(jnp.logical_not(rises))(lambda: run(False))
        return 0

    groups = count // per
    lax.fori_loop(0, groups, group, 0)
    for x in range(nx):
        for cs in cuts:
            total = 0.0
            for hs in bands:
                total = total + base_tile(cols, material[x : x + 1, cs], hs) * acc[x, hs, cs]
            gradient[x : x + 1, cs] = sub_sum(total) * 0.8
    for turn in range(groups * (nx - 1))[-slots:]:
        sent(0, 0, turn % slots).wait()


def last_kernel(
    dirs, cols, density, material, halo0_a, halo0_b, halo1_a, halo1_b, excess, edge_dual, known, gradient, dual_in,
    dual, out, done, sems,
):
    nx, plane = density.shape
    count, nb = edge_dual.shape[:2]
    half = count // 2
    cuts, bands = tiles(plane), halves(nb)
    params = halo0_a.shape[0] - SUB
    block = lax.axis_index("dir")
    even = is_even()
    copies = []
    gains = []
    for part, (halo0, halo1) in enumerate(((halo0_a, halo1_a), (halo0_b, halo1_b))):
        ahead = even if part == 0 else jnp.logical_not(even)
        first, x = jnp.where(ahead, 0, half), jnp.where(ahead, nx - 1, 0)

        def pick(ref, i, k, cs):
            return jnp.where(ahead, ref[i : i + 1, cs], ref[k : k + 1, cs])

        sums = []
        for cs in cuts:
            dens, mat = pick(density, nx - 1, 0, cs), pick(material, nx - 1, 0, cs)
            beyond = halo0[params + 1 : params + 2, cs]
            beyond_mat = halo0[params + 2 : params + 3, cs].astype(jnp.int32)
            level, drive = pick(known, 0, 1, cs), pick(known, 2, 3, cs)
            share = 0.0
            for h, hs in enumerate(bands):
                pace, base = cols[0, hs], base_tile(cols, mat, hs)
                r, r_beyond = base * (0.2 + 0.8 * dens), rate_tile(cols, beyond, beyond_mat, hs)
                source = cols[1, hs] * drive

                def add(d, total):
                    ax, ay, az = [jnp.abs(a) for a in cosines(dirs, block * count + first + d)]
                    speeds, cx = pace * (ax + ay + az), pace * ax
                    rows = pl.ds(pl.multiple_of(d * nb + h * SUB, SUB), SUB)
                    v = halo1[rows, cs] + source * inverse(speeds + r_beyond)
                    new = (cx * v) * inverse(speeds + r)
                    done[first + d, hs, cs] = edge_dual[first + d, hs, cs] + new
                    return total + new * (excess[first + d, x, hs, cs] - level)

                total = lax.fori_loop(0, half, add, jnp.zeros((SUB, LANES), jnp.float32), unroll=True)
                share = share + base * total
            sums.append(sub_sum(share) * 0.8)
        gains.append(sums)
        copy = pltpu.make_async_copy(done.at[pl.ds(first, half)], dual.at[pl.ds(first, half), x], sems.at[part])
        copy.start()
        copies.append(copy)
    out[...] = gradient[...]
    for j, cs in enumerate(cuts):
        out[nx - 1 : nx, cs] = out[nx - 1 : nx, cs] + jnp.where(even, gains[0][j], gains[1][j])
        out[0:1, cs] = out[0:1, cs] + jnp.where(even, gains[1][j], gains[0][j])
    for copy in copies:
        copy.wait()


def swapped(value, start):
    count = lax.axis_size("space")
    pairs = [(s, s + 1) for s in range(start, count - 1, 2)]
    return lax.ppermute(value, "space", pairs + [(b, a) for a, b in pairs])


def others(value, axis):
    count = lax.axis_size(axis)
    pairs = count & (count - 1) == 0
    hops = [[(s, s ^ k if pairs else (s + k) % count) for s in range(count)] for k in range(1, count)]
    return [lax.ppermute(value, axis, hop) for hop in hops]


def shares(partial, first, then):
    total = sum(others(partial, first), partial)
    return [total] + others(total, then)


def packed(parts, count):
    parts = parts + [jnp.zeros_like(parts[0])] * (count - len(parts))
    return parts[: count - 1] + [sum(parts[count:], parts[count - 1])]


def on_device(
    adjoint_start, primal_deviations, density, material, rate_table, group_speed, heat_capacity, objective_weight
):
    count, nb, nx, plane = adjoint_start.shape
    half = count // 2
    first_steps = count // math.gcd(FIRST_GROUP, half)
    second_steps = count // math.gcd(SECOND_GROUP, half)
    nmat = rate_table.shape[0]
    start = adjoint_start.transpose(0, 2, 1, 3)
    excess = primal_deviations.transpose(0, 2, 1, 3)
    f32 = jnp.float32
    vmem = pl.BlockSpec(memory_space=pltpu.VMEM)
    smem = pl.BlockSpec(memory_space=pltpu.SMEM)
    vmem = pl.BlockSpec(memory_space=pltpu.VMEM)
    hbm = pl.BlockSpec(memory_space=pltpu.HBM)
    dirs = jnp.asarray(direction_table(count))
    params = pltpu.CompilerParams(vmem_limit_bytes=VMEM_LIMIT)
    size = count * nb * nx * plane

    def stay(*arrays):
        return [pltpu.with_memory_space_constraint(a, pltpu.HBM) for a in arrays]

    def like(*shape):
        return jax.ShapeDtypeStruct(shape, f32)

    def cost(work, moved):
        return pl.CostEstimate(flops=int(size * work), bytes_accessed=int(size * moved), transcendentals=0)

    small = (heat_capacity.reshape(1, -1), group_speed.reshape(1, -1), rate_table)
    cells = (density, material, objective_weight)
    face_a, face_b, cols, density, material, objective = pl.pallas_call(
        faces_kernel,
        out_shape=(
            like(half * nb + SUB, plane), like(half * nb + SUB, plane), like(2 + nmat, nb, LANES),
            *(jax.ShapeDtypeStruct(a.shape, a.dtype) for a in cells),
        ),
        in_specs=[hbm] * 7,
        out_specs=[vmem] * 6,
        scratch_shapes=[pltpu.VMEM(a.shape, a.dtype) for a in small]
        + [pltpu.VMEM((2, half, nb, plane), f32), pltpu.SemaphoreType.DMA((6 + 2 * (half + 1),))],
        compiler_params=params,
        cost_estimate=cost(0.3, 2),
        name="faces",
    )(*stay(*small, *cells, start))
    halo0_a, halo0_b = swapped(face_a, 0), swapped(face_b, 1)

    flow, excess, face_a, face_b, sums = pl.pallas_call(
        first_kernel,
        out_shape=(
            like(*start.shape), like(*start.shape), like(half * nb, plane), like(half * nb, plane), like(4 * nx, plane)
        ),
        in_specs=[smem] + [vmem] * 3 + [hbm] * 2,
        out_specs=[vmem] * 5,
        scratch_shapes=[
            pltpu.VMEM(start.shape, f32), pltpu.VMEM((nx, nb, plane), f32), pltpu.VMEM((4, nx, nb, plane), f32),
            pltpu.SemaphoreType.DMA((2, nx)),
        ],
        compiler_params=params,
        cost_estimate=cost(20, 12),
        name="first",
    )(dirs, cols, density, material, *stay(start, excess))
    halo1_a, halo1_b = swapped(face_a, 0), swapped(face_b, 1)

    parts = packed(shares(sums, "band", "dir"), 4)

    extra = pl.pallas_call(
        edges_kernel,
        out_shape=like(SUB, plane),
        in_specs=[smem] + [vmem] * 5,
        out_specs=vmem,
        compiler_params=params,
        cost_estimate=cost(1, 1),
        name="edges",
    )(dirs, cols, density, material, halo0_a, halo0_b)
    extras = packed(shares(extra, "band", "dir"), 4)

    per = math.gcd(SECOND_GROUP, half)
    layer = pltpu.VMEM((nx, nb, plane), f32)
    rows = pltpu.VMEM((per, nb, plane), f32)
    dual, edge_dual, known, gradient = pl.pallas_call(
        second_kernel,
        out_shape=(pltpu.HBM(start.shape, f32), like(count, nb, plane), like(SUB, plane), like(nx, plane)),
        in_specs=[smem] + [vmem] * 16,
        out_specs=[hbm] + [vmem] * 3,
        scratch_shapes=[
            layer, layer, layer, pltpu.VMEM((nx, SUB, plane), f32), rows, rows, layer,
            pltpu.VMEM((SLOTS, per, nb, plane), f32), pltpu.SemaphoreType.DMA((SLOTS,)),
        ],
        compiler_params=params,
        cost_estimate=cost(30, 12),
        name="second",
    )(dirs, cols, density, material, objective, *parts, *extras, halo0_a, halo0_b, flow, excess)

    dual, gradient = pl.pallas_call(
        last_kernel,
        out_shape=(like(*start.shape), like(nx, plane)),
        in_specs=[smem] + [vmem] * 11 + [hbm],
        out_specs=[hbm, vmem],
        scratch_shapes=[pltpu.VMEM((count, nb, plane), f32), pltpu.SemaphoreType.DMA((2,))],
        input_output_aliases={12: 0},
        compiler_params=params,
        cost_estimate=cost(1, 1),
        name="last",
    )(dirs, cols, density, material, halo0_a, halo0_b, halo1_a, halo1_b, excess, edge_dual, known, gradient, dual)
    gradient = sum(shares(gradient, "band", "dir")) * (-0.125 / ITERS)
    return (dual.transpose(0, 2, 1, 3), gradient)


def solution(mesh):
    placed = (
        P("dir", "band", "space", None),
        P("dir", "band", "space", None),
        P("space", None),
        P("space", None),
        P(None, "band"),
        P("band"),
        P(),
        P("space", None),
    )
    return jax.shard_map(
        on_device,
        mesh=mesh,
        in_specs=placed,
        out_specs=(P("dir", "band", "space", None), P("space", None)),
        check_vma=False,
    )
```

```python
import math

import jax
import jax.numpy as jnp
import numpy as np
from jax import lax
from jax.experimental import pallas as pl
from jax.experimental.pallas import tpu as pltpu
from jax.sharding import PartitionSpec as P

NDIR = 64
NB = 32
NY = 192
ITERS = 2
LANES = 128
SUB = 8
FIRST_GROUP = 8
SECOND_GROUP = 8
SLOTS = 5
VMEM_LIMIT = 18 * 1024 * 1024


def direction_table(count):
    d = np.arange(NDIR)
    half = count // 2
    block, slot = d // count, d % count
    side, pair = slot // half, slot % half
    azimuth = np.pi * (block * half + pair + 0.5) / (NDIR // 2) - np.pi / 2
    along_z = 0.4 * (1.0 - 2.0 * (pair % 2))
    tilt = np.sqrt(1.0 - along_z * along_z)
    along_x = (1.0 - 2.0 * side) * tilt * np.cos(azimuth)
    along_y = tilt * np.sin(azimuth)
    return np.stack([along_x, along_y, along_z], axis=1).astype(np.float32).reshape(-1)


def lane_ids():
    return lax.broadcasted_iota(jnp.int32, (SUB, LANES), 1)


def lazily(make):
    made = {}

    def get(j):
        if j not in made:
            made[j] = make(j)
        return made[j]

    return get


def shifted(v, n, offset, lane, masked=None):
    q, rem = divmod(offset, LANES)
    zero = jnp.zeros((SUB, LANES), jnp.float32)
    rolled = lazily(lambda j: pltpu.roll(v(j), LANES - rem, 1) if rem else v(j))

    def tile(j):
        parts = []
        for k, low, high in ((j + q, 0, LANES - rem), (j + q + 1, LANES - rem, LANES)):
            kept = low < high and 0 <= k < n
            kept = kept and not all(masked is not None and masked(j * LANES + i) for i in range(low, high))
            parts.append(rolled(k) if kept else None)
        if parts[0] is None and parts[1] is None:
            return None
        t = parts[0]
        if rem:
            t = jnp.where(lane < LANES - rem, *[zero if part is None else part for part in parts])
        for i in range(LANES):
            if masked is not None and masked(j * LANES + i) and parts[int(i >= LANES - rem)] is not None:
                t = jnp.where(lane == i, zero, t)
        return t

    return lazily(tile)


def shift_y(v, n, rising, lane):
    if rising:
        return shifted(v, n, 1, lane, lambda p: p % NY == NY - 1)
    return shifted(v, n, -1, lane, lambda p: p % NY == 0)


def shift_z(v, n, rising, lane):
    return shifted(v, n, NY if rising else -NY, lane)


def inverse(x):
    r = pl.reciprocal(x, approx=True)
    return r * (2.0 - x * r)


def column(row, offset, n):
    shape = (n, row.shape[1])
    i0 = lax.broadcasted_iota(jnp.int32, shape, 0)
    i1 = lax.broadcasted_iota(jnp.int32, shape, 1)
    picked = jnp.sum(jnp.where(i1 == i0 + offset, row, 0.0), axis=1, keepdims=True)
    return jnp.broadcast_to(picked, (n, LANES))


def fill_columns(cols, heat, speed, table):
    nb = cols.shape[1]
    row = heat[...]
    total = jnp.sum(row, axis=1, keepdims=True) * float(NDIR)
    cols[0] = column(speed[...], 0, nb)
    cols[1] = column(row / total, lax.axis_index("band") * nb, nb)
    for m in range(table.shape[0]):
        cols[2 + m] = column(table[m : m + 1], 0, nb)


def rate_tile(cols, density, material, hs):
    return base_tile(cols, material, hs) * (0.2 + 0.8 * density)


def base_tile(cols, material, hs):
    base = jnp.broadcast_to(cols[2, hs], (SUB, LANES))
    for m in range(1, cols.shape[0] - 2):
        base = jnp.where(material == m, cols[2 + m, hs], base)
    return base


def halves(nb):
    return [slice(h * SUB, (h + 1) * SUB) for h in range(nb // SUB)]


def tiles(plane):
    return [slice(j * LANES, (j + 1) * LANES) for j in range(plane // LANES)]


def sub_sum(t):
    return jnp.sum(t, axis=0, keepdims=True)


def add_terms(terms):
    terms = [t for t in terms if t is not None]
    total = terms[0]
    for t in terms[1:]:
        total = total + t
    return total


def times(a, b):
    return None if b is None else a * b


def cosines(dirs, d):
    at = 3 * d
    return dirs[at], dirs[at + 1], dirs[at + 2]


def has_low():
    return lax.axis_index("band") % 2 == 0


def is_even():
    return lax.axis_index("space") % 2 == 0


def faces_kernel(
    heat_in, speed_in, table_in, density_in, material_in, objective_in, start,
    out_a, out_b, cols, density, material, objective,
    heat, speed, table, others, sems,
):
    half, nb, plane = others.shape[1:]
    last = density.shape[0] - 1
    even = is_even()
    copies = []
    for n, (src, dst) in enumerate(
        (
            (heat_in, heat), (speed_in, speed), (table_in, table),
            (density_in, density), (material_in, material), (objective_in, objective),
        )
    ):
        copies.append(pltpu.make_async_copy(src, dst, sems.at[n]))
    for side, out in enumerate((out_a, out_b)):
        upper = even if side == 0 else jnp.logical_not(even)
        first, second, x = jnp.where(upper, half, 0), jnp.where(upper, 0, half), jnp.where(upper, last, 0)
        at = 6 + side * (half + 1)
        for d in range(half):
            copies.append(
                pltpu.make_async_copy(start.at[first + d, x], out.at[pl.ds(d * nb, nb)], sems.at[at + d])
            )
        copies.append(pltpu.make_async_copy(start.at[pl.ds(second, half), x], others.at[side], sems.at[at + half]))
    for copy in copies:
        copy.start()
    for copy in copies:
        copy.wait()
    fill_columns(cols, heat, speed, table)
    for side, out in enumerate((out_a, out_b)):
        upper = even if side == 0 else jnp.logical_not(even)
        row = lambda ref, cs: jnp.where(upper, ref[last : last + 1, cs], ref[0:1, cs])
        base = half * nb
        for cs in tiles(plane):
            dens, mat = row(density, cs), row(material, cs)
            share = 0.0
            for h, hs in enumerate(halves(nb)):
                total = others[side, 0, hs, cs]
                for d in range(1, half):
                    total = total + others[side, d, hs, cs]
                for d in range(half):
                    total = total + out[d * nb + h * SUB : d * nb + (h + 1) * SUB, cs]
                share = share + rate_tile(cols, dens, mat, hs) * total
            out[base : base + 1, cs] = sub_sum(share)
            out[base + 1 : base + 2, cs] = dens
            out[base + 2 : base + 3, cs] = mat.astype(jnp.float32)
            out[base + 3 : base + 4, cs] = row(objective, cs)
            out[base + 4 : base + 8, cs] = jnp.zeros((4, LANES), jnp.float32)


def first_kernel(
    dirs, cols, density, material, start, excess_in, flow, excess, face_a, face_b, keep, give, field, rate, acc, sums, sems
):
    count, nx, nb, plane = field.shape
    half = count // 2
    per = math.gcd(FIRST_GROUP, half)
    groups = count // per
    cuts, bands = tiles(plane), halves(nb)
    n = len(cuts)

    def fetch(x, which):
        src, dst = ((start, field), (excess_in, excess))[which]
        return pltpu.make_async_copy(src.at[:, x], dst.at[:, x], sems.at[which, x])

    for x, which in ((0, 0), (1, 0), (0, 1), (2, 0), (1, 1)):
        if x < nx:
            fetch(x, which).start()
    for x in range(nx):
        for cs in cuts:
            for hs in bands:
                rate[x, hs, cs] = rate_tile(cols, density[x : x + 1, cs], material[x : x + 1, cs], hs)
    acc[...] = jnp.zeros_like(acc)
    block = lax.axis_index("dir")
    lane = lane_ids()
    fetch(0, 0).wait()

    def layer(x, _):
        pl.when(x + 3 < nx)(lambda: fetch(x + 3, 0).start())
        pl.when(x + 2 < nx)(lambda: fetch(x + 2, 1).start())
        pl.when(x + 1 < nx)(lambda: fetch(x + 1, 0).wait())
        fetch(x, 1).wait()

        def group(k, _):
            first = k * per
            ahead = first < half
            edge = jnp.where(ahead, x == nx - 1, x == 0)
            beside = jnp.where(edge, x, jnp.where(ahead, x + 1, x - 1))

            def run(rising):
                for hs in bands:
                    pace = cols[0, hs]
                    ways = []
                    for dd in range(per):
                        ax, ay, az = [jnp.abs(a) for a in cosines(dirs, block * count + first + dd)]
                        v = lazily(lambda j, dd=dd: field[first + dd, x, hs, cuts[j]])
                        speeds = (pace * jnp.where(edge, 0.0, ax), pace * ay, pace * az, pace * (ax + ay + az))
                        ways.append((v, shift_y(v, n, rising, lane), shift_z(v, n, dd % 2 == 0, lane), speeds))
                    for j, cs in enumerate(cuts):
                        r = rate[x, hs, cs]
                        kept = []
                        for dd, (v, along_y, along_z, (cx, cy, cz, speeds)) in enumerate(ways):
                            d = first + dd
                            inv = inverse(speeds + r)
                            a = inv * add_terms(
                                [times(cx, field[d, beside, hs, cs]), times(cy, along_y(j)), times(cz, along_z(j))]
                            )
                            flow[d, x, hs, cs] = a
                            kept.append((v(j), excess[d, x, hs, cs], a, inv))
                        for f in range(4):
                            acc[f, x, hs, cs] += add_terms([k[f] for k in kept])

            rises = cosines(dirs, block * count + first)[1] > 0
            pl.when(rises)(lambda: run(True))
            pl.when(jnp.logical_not(rises))(lambda: run(False))
            return 0

        lax.fori_loop(0, groups, group, 0)
        return 0

    lax.fori_loop(0, nx, layer, 0)
    even = is_even()
    for face, upper in ((face_a, even), (face_b, jnp.logical_not(even))):
        first, x = jnp.where(upper, half, 0), jnp.where(upper, nx - 1, 0)
        for d in range(half):
            face[d * nb : (d + 1) * nb] = flow[first + d, x]
    for x in range(nx):
        for cs in cuts:
            totals = [0.0] * 4
            for hs in bands:
                r, w = rate[x, hs, cs], cols[1, hs]
                for f, scale in enumerate((r, w, r, r * w)):
                    totals[f] = totals[f] + scale * acc[f, x, hs, cs]
            for f in range(4):
                sums[f * nx + x : f * nx + x + 1, cs] = sub_sum(totals[f])
    mid = 2 * nx

    def deal(low, high):
        for k, part in enumerate((low, high)):
            part[:mid] = sums[k * mid : (k + 1) * mid]
            part[mid:] = jnp.zeros((part.shape[0] - mid, plane), jnp.float32)

    pl.when(has_low())(lambda: deal(keep, give))
    pl.when(jnp.logical_not(has_low()))(lambda: deal(give, keep))


def edges_kernel(dirs, cols, density, material, halo_a, halo_b, sums, out):
    nx, plane = density.shape
    nb = cols.shape[1]
    half = (halo_a.shape[0] - SUB) // nb
    count = 2 * half
    block = lax.axis_index("dir")
    even = is_even()
    cuts = tiles(plane)
    gains = []
    for side, halo in enumerate((halo_a, halo_b)):
        ahead = even if side == 0 else jnp.logical_not(even)
        rates = []
        for hs in halves(nb):
            rates.append([])
            for cs in cuts:
                mat = jnp.where(ahead, material[nx - 1 : nx, cs], material[0:1, cs])
                dens = jnp.where(ahead, density[nx - 1 : nx, cs], density[0:1, cs])
                rates[-1].append(rate_tile(cols, dens, mat, hs))
        first = block * count + jnp.where(ahead, 0, half)

        def add(d, totals):
            ax, ay, az = [jnp.abs(a) for a in cosines(dirs, first + d)]
            new = list(totals)
            for h, hs in enumerate(halves(nb)):
                pace = cols[0, hs]
                cx, speeds = pace * ax, pace * (ax + ay + az)
                rows = halo.at[pl.ds(pl.multiple_of(d * nb + h * SUB, SUB), SUB)]
                for j, cs in enumerate(cuts):
                    r = rates[h][j]
                    new[j] = new[j] + (cx * rows[:, cs]) * (r * inverse(speeds + r))
            return tuple(new)

        totals = lax.fori_loop(0, half, add, tuple(jnp.zeros((SUB, LANES), jnp.float32) for _ in cuts))
        gains.append([sub_sum(t) for t in totals])
    base = half * nb
    row = 2 * nx
    out[...] = sums[...]
    for side in range(2):
        near, far = (0, 1) if side == 0 else (1, 0)
        for j, cs in enumerate(cuts):
            out[row + side : row + side + 1, cs] = jnp.where(even, gains[near][j], gains[far][j])
            a, b = halo_a[base : base + 1, cs], halo_b[base : base + 1, cs]
            out[row + 2 + side : row + 3 + side, cs] = jnp.where(even, a, b) if side == 0 else jnp.where(even, b, a)


def second_kernel(
    dirs, cols, density, material, objective, mine, theirs, halo0_a, halo0_b, flow, excess,
    dual, edge_dual, known, gradient,
    rate, source0, source1, warm, prev, seed, acc, stage, full, sems,
):
    count, nx, nb, plane = flow.shape
    half = count // 2
    per = prev.shape[0]
    slots = stage.shape[0]
    cuts, bands = tiles(plane), halves(nb)
    n = len(cuts)
    scale = float(NDIR * NB)
    edge = halo0_a.shape[0] - SUB
    even = is_even()

    mid = 2 * nx

    def join(low, high):
        full[:mid] = low[:mid]
        full[mid : 2 * mid] = high[:mid]
        full[2 * mid : 2 * mid + 4] = low[mid : mid + 4] + high[mid : mid + 4]

    pl.when(has_low())(lambda: join(mine, theirs))
    pl.when(jnp.logical_not(has_low()))(lambda: join(theirs, mine))
    total = full[...]
    for x in range(nx):
        warm[x] = jnp.broadcast_to(total[nx + x : nx + x + 1], (SUB, plane))
    known[0:1] = total[2 * nx - 1 : 2 * nx]
    known[1:2] = total[nx : nx + 1]
    for side in range(2):
        from_a = even if side == 0 else jnp.logical_not(even)
        aim = jnp.where(from_a, halo0_a[edge + 3 : edge + 4], halo0_b[edge + 3 : edge + 4])
        known[2 + side : 3 + side] = total[4 * nx + 2 + side : 4 * nx + 3 + side] + scale * aim
    known[4:8] = jnp.zeros((4, plane), jnp.float32)
    for x in range(nx):
        for cs in cuts:
            drive = total[x : x + 1, cs] + scale * objective[x : x + 1, cs]
            again = (
                total[2 * nx + x : 2 * nx + x + 1, cs]
                + drive * total[3 * nx + x : 3 * nx + x + 1, cs]
                + scale * objective[x : x + 1, cs]
            )
            for side, outer in enumerate((nx - 1, 0)):
                if x == outer:
                    again = again + total[4 * nx + side : 4 * nx + side + 1, cs]
            for hs in bands:
                w = cols[1, hs]
                rate[x, hs, cs] = rate_tile(cols, density[x : x + 1, cs], material[x : x + 1, cs], hs)
                source0[x, hs, cs] = w * drive
                source1[x, hs, cs] = w * again
    acc[...] = jnp.zeros_like(acc)
    block = lax.axis_index("dir")
    lane = lane_ids()

    def sent(first, x, slot):
        return pltpu.make_async_copy(stage.at[slot], dual.at[pl.ds(first, per), x], sems.at[slot])

    def group(k, _):
        first = k * per
        ahead = first < half

        def enter(halo0):
            skip = jnp.where(ahead, 0, half)
            for dd in range(per):
                ax = jnp.abs(cosines(dirs, block * count + first + dd)[0])
                for h, hs in enumerate(bands):
                    cx = cols[0, hs] * ax
                    rows = pl.ds(pl.multiple_of((first - skip + dd) * nb + h * SUB, SUB), SUB)
                    for cs in cuts:
                        seed[dd, hs, cs] = cx * halo0[rows, cs]

        pl.when(ahead == even)(lambda: enter(halo0_a))
        pl.when(ahead != even)(lambda: enter(halo0_b))

        def run(rising):
            def layer(i, at_edge):
                x = jnp.where(ahead, nx - 1 - i, i)
                turn = k * (nx - 1) + i - 1
                slot = turn % slots
                if not at_edge:
                    pl.when(turn >= slots)(lambda: sent(first, x, slot).wait())
                for hs in bands:
                    pace = cols[0, hs]
                    rates = lazily(lambda j: rate[x, hs, cuts[j]])
                    sources = lazily(lambda j: source0[x, hs, cuts[j]])
                    ways = []
                    for dd in range(per):
                        ax, ay, az = [jnp.abs(a) for a in cosines(dirs, block * count + first + dd)]
                        speeds = pace * (ax + ay + az)
                        inv = lazily(lambda j, speeds=speeds: inverse(speeds + rates(j)))

                        def fresh(j, dd=dd, inv=inv):
                            s = sources(j)
                            if at_edge:
                                s = s + seed[dd, hs, cuts[j]]
                            return flow[first + dd, x, hs, cuts[j]] + s * inv(j)

                        v = lazily(fresh)
                        shifts = (shift_y(v, n, rising, lane), shift_z(v, n, dd % 2 == 0, lane))
                        ways.append((v, inv, *shifts, (pace * ax, pace * ay, pace * az)))
                    for j, cs in enumerate(cuts):
                        kept = []
                        again, level = source1[x, hs, cs], warm[x, :, cs]
                        for dd, (v, inv, along_y, along_z, (cx, cy, cz)) in enumerate(ways):
                            beside = None if at_edge else cx * prev[dd, hs, cs]
                            new = inv(j) * add_terms([beside, times(cy, along_y(j)), times(cz, along_z(j)), again])
                            prev[dd, hs, cs] = v(j)
                            if at_edge:
                                edge_dual[first + dd, hs, cs] = new
                            else:
                                stage[slot, dd, hs, cs] = new
                            kept.append((v(j) + new) * (excess[first + dd, x, hs, cs] - level))
                        acc[x, hs, cs] += add_terms(kept)
                if not at_edge:
                    sent(first, x, slot).start()

            layer(0, True)

            def later(i, _):
                layer(i, False)
                return 0

            lax.fori_loop(1, nx, later, 0)

        rises = cosines(dirs, block * count + first)[1] > 0
        pl.when(rises)(lambda: run(True))
        pl.when(jnp.logical_not(rises))(lambda: run(False))
        return 0

    groups = count // per
    lax.fori_loop(0, groups, group, 0)
    for x in range(nx):
        for cs in cuts:
            total = 0.0
            for hs in bands:
                total = total + base_tile(cols, material[x : x + 1, cs], hs) * acc[x, hs, cs]
            gradient[x : x + 1, cs] = sub_sum(total) * 0.8
    for turn in range(groups * (nx - 1))[-slots:]:
        sent(0, 0, turn % slots).wait()


def last_kernel(
    dirs, cols, density, material, halo0_a, halo0_b, halo1_a, halo1_b, excess, edge_dual, known, gradient, dual_in,
    dual, out, done, gained, sems,
):
    nx, plane = density.shape
    count, nb = edge_dual.shape[:2]
    half = count // 2
    cuts, bands = tiles(plane), halves(nb)
    params = halo0_a.shape[0] - SUB
    block = lax.axis_index("dir")
    even = is_even()
    copies = []
    gains = []
    parts = ((halo0_a, halo1_a, even), (halo0_b, halo1_b, jnp.logical_not(even)))

    def places(ahead):
        return jnp.where(ahead, 0, half), jnp.where(ahead, nx - 1, 0)

    def pick(ahead, ref, i, k, cs):
        return jnp.where(ahead, ref[i : i + 1, cs], ref[k : k + 1, cs])

    for part, (halo0, halo1, ahead) in enumerate(parts):
        first, x = places(ahead)
        for cs in cuts:
            dens, mat = pick(ahead, density, nx - 1, 0, cs), pick(ahead, material, nx - 1, 0, cs)
            beyond = halo0[params + 1 : params + 2, cs]
            beyond_mat = halo0[params + 2 : params + 3, cs].astype(jnp.int32)
            drive = pick(ahead, known, 2, 3, cs)
            for h, hs in enumerate(bands):
                pace = cols[0, hs]
                r, r_beyond = rate_tile(cols, dens, mat, hs), rate_tile(cols, beyond, beyond_mat, hs)
                source = cols[1, hs] * drive
                for d in range(half):
                    ax, ay, az = [jnp.abs(a) for a in cosines(dirs, block * count + first + d)]
                    speeds = pace * (ax + ay + az)
                    v = halo1[d * nb + h * SUB : d * nb + (h + 1) * SUB, cs] + source * inverse(speeds + r_beyond)
                    gain = (pace * ax * v) * inverse(speeds + r)
                    gained[first + d, hs, cs] = gain
                    done[first + d, hs, cs] = edge_dual[first + d, hs, cs] + gain
        copy = pltpu.make_async_copy(done.at[pl.ds(first, half)], dual.at[pl.ds(first, half), x], sems.at[part])
        copy.start()
        copies.append(copy)
    for _, _, ahead in parts:
        first, x = places(ahead)
        sums = []
        for cs in cuts:
            mat, level = pick(ahead, material, nx - 1, 0, cs), pick(ahead, known, 0, 1, cs)
            share = 0.0
            for hs in bands:
                total = add_terms(
                    [gained[first + d, hs, cs] * (excess[first + d, x, hs, cs] - level) for d in range(half)]
                )
                share = share + base_tile(cols, mat, hs) * total
            sums.append(sub_sum(share) * 0.8)
        gains.append(sums)
    out[...] = gradient[...]
    for j, cs in enumerate(cuts):
        out[nx - 1 : nx, cs] = out[nx - 1 : nx, cs] + jnp.where(even, gains[0][j], gains[1][j])
        out[0:1, cs] = out[0:1, cs] + jnp.where(even, gains[1][j], gains[0][j])
    for copy in copies:
        copy.wait()


def swapped(value, start):
    count = lax.axis_size("space")
    pairs = [(s, s + 1) for s in range(start, count - 1, 2)]
    return lax.ppermute(value, "space", pairs + [(b, a) for a, b in pairs])


def others(value, axis):
    count = lax.axis_size(axis)
    pairs = count & (count - 1) == 0
    hops = [[(s, s ^ k if pairs else (s + k) % count) for s in range(count)] for k in range(1, count)]
    return [lax.ppermute(value, axis, hop) for hop in hops]


def shares(value, axis):
    return [value] + others(value, axis)


def on_device(
    adjoint_start, primal_deviations, density, material, rate_table, group_speed, heat_capacity, objective_weight
):
    count, nb, nx, plane = adjoint_start.shape
    half = count // 2
    first_steps = count // math.gcd(FIRST_GROUP, half)
    second_steps = count // math.gcd(SECOND_GROUP, half)
    nmat = rate_table.shape[0]
    start = adjoint_start.transpose(0, 2, 1, 3)
    excess = primal_deviations.transpose(0, 2, 1, 3)
    f32 = jnp.float32
    vmem = pl.BlockSpec(memory_space=pltpu.VMEM)
    smem = pl.BlockSpec(memory_space=pltpu.SMEM)
    vmem = pl.BlockSpec(memory_space=pltpu.VMEM)
    hbm = pl.BlockSpec(memory_space=pltpu.HBM)
    dirs = jnp.asarray(direction_table(count))
    params = pltpu.CompilerParams(vmem_limit_bytes=VMEM_LIMIT)
    size = count * nb * nx * plane

    def stay(*arrays):
        return [pltpu.with_memory_space_constraint(a, pltpu.HBM) for a in arrays]

    def like(*shape):
        return jax.ShapeDtypeStruct(shape, f32)

    def cost(work, moved):
        return pl.CostEstimate(flops=int(size * work), bytes_accessed=int(size * moved), transcendentals=0)

    small = (heat_capacity.reshape(1, -1), group_speed.reshape(1, -1), rate_table)
    cells = (density, material, objective_weight)
    face_a, face_b, cols, density, material, objective = pl.pallas_call(
        faces_kernel,
        out_shape=(
            like(half * nb + SUB, plane), like(half * nb + SUB, plane), like(2 + nmat, nb, LANES),
            *(jax.ShapeDtypeStruct(a.shape, a.dtype) for a in cells),
        ),
        in_specs=[hbm] * 7,
        out_specs=[vmem] * 6,
        scratch_shapes=[pltpu.VMEM(a.shape, a.dtype) for a in small]
        + [pltpu.VMEM((2, half, nb, plane), f32), pltpu.SemaphoreType.DMA((6 + 2 * (half + 1),))],
        compiler_params=params,
        cost_estimate=cost(0.3, 2),
        name="faces",
    )(*stay(*small, *cells, start))
    halo0_a, halo0_b = swapped(face_a, 0), swapped(face_b, 1)

    mid = -(-(2 * nx + 4) // SUB) * SUB
    flow, excess, face_a, face_b, keep, give = pl.pallas_call(
        first_kernel,
        out_shape=(
            like(*start.shape), like(*start.shape), like(half * nb, plane), like(half * nb, plane),
            like(mid, plane), like(mid, plane),
        ),
        in_specs=[smem] + [vmem] * 3 + [hbm] * 2,
        out_specs=[vmem] * 6,
        scratch_shapes=[
            pltpu.VMEM(start.shape, f32), pltpu.VMEM((nx, nb, plane), f32), pltpu.VMEM((4, nx, nb, plane), f32),
            pltpu.VMEM((4 * nx, plane), f32), pltpu.SemaphoreType.DMA((2, nx)),
        ],
        compiler_params=params,
        cost_estimate=cost(20, 12),
        name="first",
    )(dirs, cols, density, material, *stay(start, excess))
    halo1_a, halo1_b = swapped(face_a, 0), swapped(face_b, 1)

    sums = pl.pallas_call(
        edges_kernel,
        out_shape=like(mid, plane),
        in_specs=[smem] + [vmem] * 6,
        out_specs=vmem,
        compiler_params=params,
        cost_estimate=cost(1, 1),
        name="edges",
    )(dirs, cols, density, material, halo0_a, halo0_b, keep + others(give, "band")[0])
    mine = sum(shares(sums, "dir"))
    theirs = others(mine, "band")[0]

    per = math.gcd(SECOND_GROUP, half)
    layer = pltpu.VMEM((nx, nb, plane), f32)
    rows = pltpu.VMEM((per, nb, plane), f32)
    dual, edge_dual, known, gradient = pl.pallas_call(
        second_kernel,
        out_shape=(pltpu.HBM(start.shape, f32), like(count, nb, plane), like(SUB, plane), like(nx, plane)),
        in_specs=[smem] + [vmem] * 10,
        out_specs=[hbm] + [vmem] * 3,
        scratch_shapes=[
            layer, layer, layer, pltpu.VMEM((nx, SUB, plane), f32), rows, rows, layer,
            pltpu.VMEM((SLOTS, per, nb, plane), f32), pltpu.VMEM((4 * nx + SUB, plane), f32),
            pltpu.SemaphoreType.DMA((SLOTS,)),
        ],
        compiler_params=params,
        cost_estimate=cost(30, 12),
        name="second",
    )(dirs, cols, density, material, objective, mine, theirs, halo0_a, halo0_b, flow, excess)

    dual, gradient = pl.pallas_call(
        last_kernel,
        out_shape=(like(*start.shape), like(nx, plane)),
        in_specs=[smem] + [vmem] * 11 + [hbm],
        out_specs=[hbm, vmem],
        scratch_shapes=[pltpu.VMEM((count, nb, plane), f32)] * 2 + [pltpu.SemaphoreType.DMA((2,))],
        input_output_aliases={12: 0},
        compiler_params=params,
        cost_estimate=cost(1, 1),
        name="last",
    )(dirs, cols, density, material, halo0_a, halo0_b, halo1_a, halo1_b, excess, edge_dual, known, gradient, dual)
    gradient = sum(shares(sum(shares(gradient, "band")), "dir")) * (-0.125 / ITERS)
    return (dual.transpose(0, 2, 1, 3), gradient)


def solution(mesh):
    placed = (
        P("dir", "band", "space", None),
        P("dir", "band", "space", None),
        P("space", None),
        P("space", None),
        P(None, "band"),
        P("band"),
        P(),
        P("space", None),
    )
    return jax.shard_map(
        on_device,
        mesh=mesh,
        in_specs=placed,
        out_specs=(P("dir", "band", "space", None), P("space", None)),
        check_vma=False,
    )
```

```python
import math

import jax
import jax.numpy as jnp
import numpy as np
from jax import lax
from jax.experimental import pallas as pl
from jax.experimental.pallas import tpu as pltpu
from jax.sharding import PartitionSpec as P

NDIR = 64
NB = 32
NY = 192
ITERS = 2
LANES = 128
SUB = 8
FIRST_GROUP = 8
SECOND_GROUP = 8
SLOTS = 5
VMEM_LIMIT = 18 * 1024 * 1024


def direction_table(count):
    d = np.arange(NDIR)
    half = count // 2
    block, slot = d // count, d % count
    side, pair = slot // half, slot % half
    azimuth = np.pi * (block * half + pair + 0.5) / (NDIR // 2) - np.pi / 2
    along_z = 0.4 * (1.0 - 2.0 * (pair % 2))
    tilt = np.sqrt(1.0 - along_z * along_z)
    along_x = (1.0 - 2.0 * side) * tilt * np.cos(azimuth)
    along_y = tilt * np.sin(azimuth)
    return np.stack([along_x, along_y, along_z], axis=1).astype(np.float32).reshape(-1)


def lane_ids():
    return lax.broadcasted_iota(jnp.int32, (SUB, LANES), 1)


def lazily(make):
    made = {}

    def get(j):
        if j not in made:
            made[j] = make(j)
        return made[j]

    return get


def shifted(v, n, offset, lane, masked=None):
    q, rem = divmod(offset, LANES)
    zero = jnp.zeros((SUB, LANES), jnp.float32)
    rolled = lazily(lambda j: pltpu.roll(v(j), LANES - rem, 1) if rem else v(j))

    def tile(j):
        parts = []
        for k, low, high in ((j + q, 0, LANES - rem), (j + q + 1, LANES - rem, LANES)):
            kept = low < high and 0 <= k < n
            kept = kept and not all(masked is not None and masked(j * LANES + i) for i in range(low, high))
            parts.append(rolled(k) if kept else None)
        if parts[0] is None and parts[1] is None:
            return None
        t = parts[0]
        if rem:
            t = jnp.where(lane < LANES - rem, *[zero if part is None else part for part in parts])
        for i in range(LANES):
            if masked is not None and masked(j * LANES + i) and parts[int(i >= LANES - rem)] is not None:
                t = jnp.where(lane == i, zero, t)
        return t

    return lazily(tile)


def shift_y(v, n, rising, lane):
    if rising:
        return shifted(v, n, 1, lane, lambda p: p % NY == NY - 1)
    return shifted(v, n, -1, lane, lambda p: p % NY == 0)


def shift_z(v, n, rising, lane):
    return shifted(v, n, NY if rising else -NY, lane)


def inverse(x):
    r = pl.reciprocal(x, approx=True)
    return r * (2.0 - x * r)


def column(row, offset, n):
    shape = (n, row.shape[1])
    i0 = lax.broadcasted_iota(jnp.int32, shape, 0)
    i1 = lax.broadcasted_iota(jnp.int32, shape, 1)
    picked = jnp.sum(jnp.where(i1 == i0 + offset, row, 0.0), axis=1, keepdims=True)
    return jnp.broadcast_to(picked, (n, LANES))


def fill_columns(cols, heat, speed, table):
    nb = cols.shape[1]
    row = heat[...]
    total = jnp.sum(row, axis=1, keepdims=True) * float(NDIR)
    cols[0] = column(speed[...], 0, nb)
    cols[1] = column(row / total, lax.axis_index("band") * nb, nb)
    for m in range(table.shape[0]):
        cols[2 + m] = column(table[m : m + 1], 0, nb)


def rate_tile(cols, density, material, hs):
    return base_tile(cols, material, hs) * (0.2 + 0.8 * density)


def base_tile(cols, material, hs):
    base = jnp.broadcast_to(cols[2, hs], (SUB, LANES))
    for m in range(1, cols.shape[0] - 2):
        base = jnp.where(material == m, cols[2 + m, hs], base)
    return base


def halves(nb):
    return [slice(h * SUB, (h + 1) * SUB) for h in range(nb // SUB)]


def tiles(plane):
    return [slice(j * LANES, (j + 1) * LANES) for j in range(plane // LANES)]


def sub_sum(t):
    return jnp.sum(t, axis=0, keepdims=True)


def add_terms(terms):
    terms = [t for t in terms if t is not None]
    total = terms[0]
    for t in terms[1:]:
        total = total + t
    return total


def times(a, b):
    return None if b is None else a * b


def cosines(dirs, d):
    at = 3 * d
    return dirs[at], dirs[at + 1], dirs[at + 2]


def has_low():
    return lax.axis_index("band") % 2 == 0


def is_even():
    return lax.axis_index("space") % 2 == 0


def faces_kernel(
    heat_in, speed_in, table_in, density_in, material_in, objective_in, start,
    out_a, out_b, cols, density, material, objective,
    heat, speed, table, others, sems,
):
    half, nb, plane = others.shape[1:]
    last = density.shape[0] - 1
    even = is_even()
    copies = []
    for n, (src, dst) in enumerate(
        (
            (heat_in, heat), (speed_in, speed), (table_in, table),
            (density_in, density), (material_in, material), (objective_in, objective),
        )
    ):
        copies.append(pltpu.make_async_copy(src, dst, sems.at[n]))
    for side, out in enumerate((out_a, out_b)):
        upper = even if side == 0 else jnp.logical_not(even)
        first, second, x = jnp.where(upper, half, 0), jnp.where(upper, 0, half), jnp.where(upper, last, 0)
        at = 6 + side * (half + 1)
        for d in range(half):
            copies.append(
                pltpu.make_async_copy(start.at[first + d, x], out.at[pl.ds(d * nb, nb)], sems.at[at + d])
            )
        copies.append(pltpu.make_async_copy(start.at[pl.ds(second, half), x], others.at[side], sems.at[at + half]))
    for copy in copies:
        copy.start()
    for copy in copies[:6]:
        copy.wait()
    fill_columns(cols, heat, speed, table)
    for side, out in enumerate((out_a, out_b)):
        upper = even if side == 0 else jnp.logical_not(even)
        row = lambda ref, cs: jnp.where(upper, ref[last : last + 1, cs], ref[0:1, cs])
        base = half * nb
        for copy in copies[6 + side * (half + 1) : 6 + (side + 1) * (half + 1)]:
            copy.wait()
        for cs in tiles(plane):
            dens, mat = row(density, cs), row(material, cs)
            share = 0.0
            for h, hs in enumerate(halves(nb)):
                total = others[side, 0, hs, cs]
                for d in range(1, half):
                    total = total + others[side, d, hs, cs]
                for d in range(half):
                    total = total + out[d * nb + h * SUB : d * nb + (h + 1) * SUB, cs]
                share = share + rate_tile(cols, dens, mat, hs) * total
            out[base : base + 1, cs] = sub_sum(share)
            out[base + 1 : base + 2, cs] = dens
            out[base + 2 : base + 3, cs] = mat.astype(jnp.float32)
            out[base + 3 : base + 4, cs] = row(objective, cs)
            out[base + 4 : base + 8, cs] = jnp.zeros((4, LANES), jnp.float32)


def first_kernel(
    dirs, cols, density, material, start, excess_in, flow, excess, face_a, face_b, keep, give, field, rate, acc, sums, sems
):
    count, nx, nb, plane = field.shape
    half = count // 2
    per = math.gcd(FIRST_GROUP, half)
    groups = count // per
    cuts, bands = tiles(plane), halves(nb)
    n = len(cuts)

    def fetch(x, which):
        src, dst = ((start, field), (excess_in, excess))[which]
        return pltpu.make_async_copy(src.at[:, x], dst.at[:, x], sems.at[which, x])

    for x, which in ((0, 0), (1, 0), (0, 1), (2, 0), (1, 1)):
        if x < nx:
            fetch(x, which).start()
    for x in range(nx):
        for cs in cuts:
            for hs in bands:
                rate[x, hs, cs] = rate_tile(cols, density[x : x + 1, cs], material[x : x + 1, cs], hs)
    acc[...] = jnp.zeros_like(acc)
    block = lax.axis_index("dir")
    lane = lane_ids()
    fetch(0, 0).wait()

    def layer(x, _):
        pl.when(x + 3 < nx)(lambda: fetch(x + 3, 0).start())
        pl.when(x + 2 < nx)(lambda: fetch(x + 2, 1).start())
        pl.when(x + 1 < nx)(lambda: fetch(x + 1, 0).wait())
        fetch(x, 1).wait()

        def group(k, _):
            first = k * per
            ahead = first < half
            edge = jnp.where(ahead, x == nx - 1, x == 0)
            beside = jnp.where(edge, x, jnp.where(ahead, x + 1, x - 1))

            def run(rising):
                for hs in bands:
                    pace = cols[0, hs]
                    ways = []
                    for dd in range(per):
                        ax, ay, az = [jnp.abs(a) for a in cosines(dirs, block * count + first + dd)]
                        v = lazily(lambda j, dd=dd: field[first + dd, x, hs, cuts[j]])
                        speeds = (pace * jnp.where(edge, 0.0, ax), pace * ay, pace * az, pace * (ax + ay + az))
                        ways.append((v, shift_y(v, n, rising, lane), shift_z(v, n, dd % 2 == 0, lane), speeds))
                    for j, cs in enumerate(cuts):
                        r = rate[x, hs, cs]
                        kept = []
                        for dd, (v, along_y, along_z, (cx, cy, cz, speeds)) in enumerate(ways):
                            d = first + dd
                            inv = inverse(speeds + r)
                            a = inv * add_terms(
                                [times(cx, field[d, beside, hs, cs]), times(cy, along_y(j)), times(cz, along_z(j))]
                            )
                            flow[d, x, hs, cs] = a
                            kept.append((v(j), excess[d, x, hs, cs], a, inv))
                        for f in range(4):
                            acc[f, x, hs, cs] += add_terms([k[f] for k in kept])

            rises = cosines(dirs, block * count + first)[1] > 0
            pl.when(rises)(lambda: run(True))
            pl.when(jnp.logical_not(rises))(lambda: run(False))
            return 0

        lax.fori_loop(0, groups, group, 0)
        return 0

    lax.fori_loop(0, nx, layer, 0)
    even = is_even()
    for face, upper in ((face_a, even), (face_b, jnp.logical_not(even))):
        first, x = jnp.where(upper, half, 0), jnp.where(upper, nx - 1, 0)
        for d in range(half):
            face[d * nb : (d + 1) * nb] = flow[first + d, x]
    for x in range(nx):
        for cs in cuts:
            totals = [0.0] * 4
            for hs in bands:
                r, w = rate[x, hs, cs], cols[1, hs]
                for f, scale in enumerate((r, w, r, r * w)):
                    totals[f] = totals[f] + scale * acc[f, x, hs, cs]
            for f in range(4):
                sums[f * nx + x : f * nx + x + 1, cs] = sub_sum(totals[f])
    mid = 2 * nx

    def deal(low, high):
        for k, part in enumerate((low, high)):
            part[:mid] = sums[k * mid : (k + 1) * mid]
            part[mid:] = jnp.zeros((part.shape[0] - mid, plane), jnp.float32)

    pl.when(has_low())(lambda: deal(keep, give))
    pl.when(jnp.logical_not(has_low()))(lambda: deal(give, keep))


def edges_kernel(dirs, cols, density, material, halo_a, halo_b, sums, out):
    nx, plane = density.shape
    nb = cols.shape[1]
    half = (halo_a.shape[0] - SUB) // nb
    count = 2 * half
    block = lax.axis_index("dir")
    even = is_even()
    cuts = tiles(plane)
    gains = []
    for side, halo in enumerate((halo_a, halo_b)):
        ahead = even if side == 0 else jnp.logical_not(even)
        rates = []
        for hs in halves(nb):
            rates.append([])
            for cs in cuts:
                mat = jnp.where(ahead, material[nx - 1 : nx, cs], material[0:1, cs])
                dens = jnp.where(ahead, density[nx - 1 : nx, cs], density[0:1, cs])
                rates[-1].append(rate_tile(cols, dens, mat, hs))
        first = block * count + jnp.where(ahead, 0, half)

        def add(d, totals):
            ax, ay, az = [jnp.abs(a) for a in cosines(dirs, first + d)]
            new = list(totals)
            for h, hs in enumerate(halves(nb)):
                pace = cols[0, hs]
                cx, speeds = pace * ax, pace * (ax + ay + az)
                rows = halo.at[pl.ds(pl.multiple_of(d * nb + h * SUB, SUB), SUB)]
                for j, cs in enumerate(cuts):
                    r = rates[h][j]
                    new[j] = new[j] + (cx * rows[:, cs]) * (r * inverse(speeds + r))
            return tuple(new)

        totals = lax.fori_loop(0, half, add, tuple(jnp.zeros((SUB, LANES), jnp.float32) for _ in cuts))
        gains.append([sub_sum(t) for t in totals])
    base = half * nb
    row = 2 * nx
    out[...] = sums[...]
    for side in range(2):
        near, far = (0, 1) if side == 0 else (1, 0)
        for j, cs in enumerate(cuts):
            out[row + side : row + side + 1, cs] = jnp.where(even, gains[near][j], gains[far][j])
            a, b = halo_a[base : base + 1, cs], halo_b[base : base + 1, cs]
            out[row + 2 + side : row + 3 + side, cs] = jnp.where(even, a, b) if side == 0 else jnp.where(even, b, a)


def second_kernel(
    dirs, cols, density, material, objective, mine, theirs, halo0_a, halo0_b, flow, excess,
    dual, edge_dual, known, gradient,
    rate, source0, source1, warm, prev, seed, acc, stage, full, sems,
):
    count, nx, nb, plane = flow.shape
    half = count // 2
    per = prev.shape[0]
    slots = stage.shape[0]
    cuts, bands = tiles(plane), halves(nb)
    n = len(cuts)
    scale = float(NDIR * NB)
    edge = halo0_a.shape[0] - SUB
    even = is_even()

    mid = 2 * nx

    def join(low, high):
        full[:mid] = low[:mid]
        full[mid : 2 * mid] = high[:mid]
        full[2 * mid : 2 * mid + 4] = low[mid : mid + 4] + high[mid : mid + 4]

    pl.when(has_low())(lambda: join(mine, theirs))
    pl.when(jnp.logical_not(has_low()))(lambda: join(theirs, mine))
    total = full[...]
    for x in range(nx):
        warm[x] = jnp.broadcast_to(total[nx + x : nx + x + 1], (SUB, plane))
    known[0:1] = total[2 * nx - 1 : 2 * nx]
    known[1:2] = total[nx : nx + 1]
    for side in range(2):
        from_a = even if side == 0 else jnp.logical_not(even)
        aim = jnp.where(from_a, halo0_a[edge + 3 : edge + 4], halo0_b[edge + 3 : edge + 4])
        known[2 + side : 3 + side] = total[4 * nx + 2 + side : 4 * nx + 3 + side] + scale * aim
    known[4:8] = jnp.zeros((4, plane), jnp.float32)
    for x in range(nx):
        for cs in cuts:
            drive = total[x : x + 1, cs] + scale * objective[x : x + 1, cs]
            again = (
                total[2 * nx + x : 2 * nx + x + 1, cs]
                + drive * total[3 * nx + x : 3 * nx + x + 1, cs]
                + scale * objective[x : x + 1, cs]
            )
            for side, outer in enumerate((nx - 1, 0)):
                if x == outer:
                    again = again + total[4 * nx + side : 4 * nx + side + 1, cs]
            for hs in bands:
                w = cols[1, hs]
                rate[x, hs, cs] = rate_tile(cols, density[x : x + 1, cs], material[x : x + 1, cs], hs)
                source0[x, hs, cs] = w * drive
                source1[x, hs, cs] = w * again
    acc[...] = jnp.zeros_like(acc)
    block = lax.axis_index("dir")
    lane = lane_ids()

    def sent(first, x, slot):
        return pltpu.make_async_copy(stage.at[slot], dual.at[pl.ds(first, per), x], sems.at[slot])

    def group(k, _):
        first = k * per
        ahead = first < half

        def enter(halo0):
            skip = jnp.where(ahead, 0, half)
            for dd in range(per):
                ax = jnp.abs(cosines(dirs, block * count + first + dd)[0])
                for h, hs in enumerate(bands):
                    cx = cols[0, hs] * ax
                    rows = pl.ds(pl.multiple_of((first - skip + dd) * nb + h * SUB, SUB), SUB)
                    for cs in cuts:
                        seed[dd, hs, cs] = cx * halo0[rows, cs]

        pl.when(ahead == even)(lambda: enter(halo0_a))
        pl.when(ahead != even)(lambda: enter(halo0_b))

        def run(rising):
            def layer(i, at_edge):
                x = jnp.where(ahead, nx - 1 - i, i)
                turn = k * (nx - 1) + i - 1
                slot = turn % slots
                if not at_edge:
                    pl.when(turn >= slots)(lambda: sent(first, x, slot).wait())
                for hs in bands:
                    pace = cols[0, hs]
                    rates = lazily(lambda j: rate[x, hs, cuts[j]])
                    sources = lazily(lambda j: source0[x, hs, cuts[j]])
                    ways = []
                    for dd in range(per):
                        ax, ay, az = [jnp.abs(a) for a in cosines(dirs, block * count + first + dd)]
                        speeds = pace * (ax + ay + az)
                        inv = lazily(lambda j, speeds=speeds: inverse(speeds + rates(j)))

                        def fresh(j, dd=dd, inv=inv):
                            s = sources(j)
                            if at_edge:
                                s = s + seed[dd, hs, cuts[j]]
                            return flow[first + dd, x, hs, cuts[j]] + s * inv(j)

                        v = lazily(fresh)
                        shifts = (shift_y(v, n, rising, lane), shift_z(v, n, dd % 2 == 0, lane))
                        ways.append((v, inv, *shifts, (pace * ax, pace * ay, pace * az)))
                    for j, cs in enumerate(cuts):
                        kept = []
                        again, level = source1[x, hs, cs], warm[x, :, cs]
                        for dd, (v, inv, along_y, along_z, (cx, cy, cz)) in enumerate(ways):
                            beside = None if at_edge else cx * prev[dd, hs, cs]
                            new = inv(j) * add_terms([beside, times(cy, along_y(j)), times(cz, along_z(j)), again])
                            prev[dd, hs, cs] = v(j)
                            if at_edge:
                                edge_dual[first + dd, hs, cs] = new
                            else:
                                stage[slot, dd, hs, cs] = new
                            kept.append((v(j) + new) * (excess[first + dd, x, hs, cs] - level))
                        acc[x, hs, cs] += add_terms(kept)
                if not at_edge:
                    sent(first, x, slot).start()

            layer(0, True)

            def later(i, _):
                layer(i, False)
                return 0

            lax.fori_loop(1, nx, later, 0)

        rises = cosines(dirs, block * count + first)[1] > 0
        pl.when(rises)(lambda: run(True))
        pl.when(jnp.logical_not(rises))(lambda: run(False))
        return 0

    groups = count // per
    lax.fori_loop(0, groups, group, 0)
    for x in range(nx):
        for cs in cuts:
            total = 0.0
            for hs in bands:
                total = total + base_tile(cols, material[x : x + 1, cs], hs) * acc[x, hs, cs]
            gradient[x : x + 1, cs] = sub_sum(total) * 0.8
    for turn in range(groups * (nx - 1))[-slots:]:
        sent(0, 0, turn % slots).wait()


def last_kernel(
    dirs, cols, density, material, halo0_a, halo0_b, halo1_a, halo1_b, excess, edge_dual, known, gradient,
    out, done, gained,
):
    nx, plane = density.shape
    count, nb = edge_dual.shape[:2]
    half = count // 2
    cuts, bands = tiles(plane), halves(nb)
    params = halo0_a.shape[0] - SUB
    block = lax.axis_index("dir")
    even = is_even()
    gains = []
    parts = ((halo0_a, halo1_a, even), (halo0_b, halo1_b, jnp.logical_not(even)))

    def places(ahead):
        return jnp.where(ahead, 0, half), jnp.where(ahead, nx - 1, 0)

    def pick(ahead, ref, i, k, cs):
        return jnp.where(ahead, ref[i : i + 1, cs], ref[k : k + 1, cs])

    for part, (halo0, halo1, ahead) in enumerate(parts):
        first, x = places(ahead)
        for cs in cuts:
            dens, mat = pick(ahead, density, nx - 1, 0, cs), pick(ahead, material, nx - 1, 0, cs)
            beyond = halo0[params + 1 : params + 2, cs]
            beyond_mat = halo0[params + 2 : params + 3, cs].astype(jnp.int32)
            drive = pick(ahead, known, 2, 3, cs)
            for h, hs in enumerate(bands):
                pace = cols[0, hs]
                r, r_beyond = rate_tile(cols, dens, mat, hs), rate_tile(cols, beyond, beyond_mat, hs)
                source = cols[1, hs] * drive
                for d in range(half):
                    ax, ay, az = [jnp.abs(a) for a in cosines(dirs, block * count + first + d)]
                    speeds = pace * (ax + ay + az)
                    v = halo1[d * nb + h * SUB : d * nb + (h + 1) * SUB, cs] + source * inverse(speeds + r_beyond)
                    gain = (pace * ax * v) * inverse(speeds + r)
                    gained[first + d, hs, cs] = gain
                    done[first + d, hs, cs] = edge_dual[first + d, hs, cs] + gain
    for _, _, ahead in parts:
        first, x = places(ahead)
        sums = []
        for cs in cuts:
            mat, level = pick(ahead, material, nx - 1, 0, cs), pick(ahead, known, 0, 1, cs)
            share = 0.0
            for hs in bands:
                total = add_terms(
                    [gained[first + d, hs, cs] * (excess[first + d, x, hs, cs] - level) for d in range(half)]
                )
                share = share + base_tile(cols, mat, hs) * total
            sums.append(sub_sum(share) * 0.8)
        gains.append(sums)
    out[...] = gradient[...]
    for j, cs in enumerate(cuts):
        out[nx - 1 : nx, cs] = out[nx - 1 : nx, cs] + jnp.where(even, gains[0][j], gains[1][j])
        out[0:1, cs] = out[0:1, cs] + jnp.where(even, gains[1][j], gains[0][j])


def place_kernel(done, dual_in, dual, sems):
    half = done.shape[0] // 2
    copies = [
        pltpu.make_async_copy(
            done.at[pl.ds(side * half, half)], dual.at[pl.ds(side * half, half), x], sems.at[side]
        )
        for side, x in enumerate((dual.shape[1] - 1, 0))
    ]
    for copy in copies:
        copy.start()
    for copy in copies:
        copy.wait()


def swapped(value, start):
    count = lax.axis_size("space")
    pairs = [(s, s + 1) for s in range(start, count - 1, 2)]
    return lax.ppermute(value, "space", pairs + [(b, a) for a, b in pairs])


def others(value, axis):
    count = lax.axis_size(axis)
    pairs = count & (count - 1) == 0
    hops = [[(s, s ^ k if pairs else (s + k) % count) for s in range(count)] for k in range(1, count)]
    return [lax.ppermute(value, axis, hop) for hop in hops]


def shares(value, axis):
    return [value] + others(value, axis)


def on_device(
    adjoint_start, primal_deviations, density, material, rate_table, group_speed, heat_capacity, objective_weight
):
    count, nb, nx, plane = adjoint_start.shape
    half = count // 2
    first_steps = count // math.gcd(FIRST_GROUP, half)
    second_steps = count // math.gcd(SECOND_GROUP, half)
    nmat = rate_table.shape[0]
    start = adjoint_start.transpose(0, 2, 1, 3)
    excess = primal_deviations.transpose(0, 2, 1, 3)
    f32 = jnp.float32
    vmem = pl.BlockSpec(memory_space=pltpu.VMEM)
    smem = pl.BlockSpec(memory_space=pltpu.SMEM)
    vmem = pl.BlockSpec(memory_space=pltpu.VMEM)
    hbm = pl.BlockSpec(memory_space=pltpu.HBM)
    dirs = jnp.asarray(direction_table(count))
    params = pltpu.CompilerParams(vmem_limit_bytes=VMEM_LIMIT)
    size = count * nb * nx * plane

    def stay(*arrays):
        return [pltpu.with_memory_space_constraint(a, pltpu.HBM) for a in arrays]

    def like(*shape):
        return jax.ShapeDtypeStruct(shape, f32)

    def cost(work, moved):
        return pl.CostEstimate(flops=int(size * work), bytes_accessed=int(size * moved), transcendentals=0)

    small = (heat_capacity.reshape(1, -1), group_speed.reshape(1, -1), rate_table)
    cells = (density, material, objective_weight)
    face_a, face_b, cols, density, material, objective = pl.pallas_call(
        faces_kernel,
        out_shape=(
            like(half * nb + SUB, plane), like(half * nb + SUB, plane), like(2 + nmat, nb, LANES),
            *(jax.ShapeDtypeStruct(a.shape, a.dtype) for a in cells),
        ),
        in_specs=[hbm] * 7,
        out_specs=[vmem] * 6,
        scratch_shapes=[pltpu.VMEM(a.shape, a.dtype) for a in small]
        + [pltpu.VMEM((2, half, nb, plane), f32), pltpu.SemaphoreType.DMA((6 + 2 * (half + 1),))],
        compiler_params=params,
        cost_estimate=cost(0.3, 2),
        name="faces",
    )(*stay(*small, *cells, start))
    halo0_a, halo0_b = swapped(face_a, 0), swapped(face_b, 1)

    mid = -(-(2 * nx + 4) // SUB) * SUB
    flow, excess, face_a, face_b, keep, give = pl.pallas_call(
        first_kernel,
        out_shape=(
            like(*start.shape), like(*start.shape), like(half * nb, plane), like(half * nb, plane),
            like(mid, plane), like(mid, plane),
        ),
        in_specs=[smem] + [vmem] * 3 + [hbm] * 2,
        out_specs=[vmem] * 6,
        scratch_shapes=[
            pltpu.VMEM(start.shape, f32), pltpu.VMEM((nx, nb, plane), f32), pltpu.VMEM((4, nx, nb, plane), f32),
            pltpu.VMEM((4 * nx, plane), f32), pltpu.SemaphoreType.DMA((2, nx)),
        ],
        compiler_params=params,
        cost_estimate=cost(20, 12),
        name="first",
    )(dirs, cols, density, material, *stay(start, excess))
    halo1_a, halo1_b = swapped(face_a, 0), swapped(face_b, 1)

    sums = pl.pallas_call(
        edges_kernel,
        out_shape=like(mid, plane),
        in_specs=[smem] + [vmem] * 6,
        out_specs=vmem,
        compiler_params=params,
        cost_estimate=cost(1, 1),
        name="edges",
    )(dirs, cols, density, material, halo0_a, halo0_b, keep + others(give, "band")[0])
    mine = sum(shares(sums, "dir"))
    theirs = others(mine, "band")[0]

    per = math.gcd(SECOND_GROUP, half)
    layer = pltpu.VMEM((nx, nb, plane), f32)
    rows = pltpu.VMEM((per, nb, plane), f32)
    dual, edge_dual, known, gradient = pl.pallas_call(
        second_kernel,
        out_shape=(pltpu.HBM(start.shape, f32), like(count, nb, plane), like(SUB, plane), like(nx, plane)),
        in_specs=[smem] + [vmem] * 10,
        out_specs=[hbm] + [vmem] * 3,
        scratch_shapes=[
            layer, layer, layer, pltpu.VMEM((nx, SUB, plane), f32), rows, rows, layer,
            pltpu.VMEM((SLOTS, per, nb, plane), f32), pltpu.VMEM((4 * nx + SUB, plane), f32),
            pltpu.SemaphoreType.DMA((SLOTS,)),
        ],
        compiler_params=params,
        cost_estimate=cost(30, 12),
        name="second",
    )(dirs, cols, density, material, objective, mine, theirs, halo0_a, halo0_b, flow, excess)

    gradient, done = pl.pallas_call(
        last_kernel,
        out_shape=(like(nx, plane), like(count, nb, plane)),
        in_specs=[smem] + [vmem] * 11,
        out_specs=[vmem] * 2,
        scratch_shapes=[pltpu.VMEM((count, nb, plane), f32)],
        compiler_params=params,
        cost_estimate=cost(1, 1),
        name="last",
    )(dirs, cols, density, material, halo0_a, halo0_b, halo1_a, halo1_b, excess, edge_dual, known, gradient)
    gradient = sum(shares(sum(shares(gradient, "band")), "dir")) * (-0.125 / ITERS)
    dual = pl.pallas_call(
        place_kernel,
        out_shape=like(*start.shape),
        in_specs=[vmem, hbm],
        out_specs=hbm,
        scratch_shapes=[pltpu.SemaphoreType.DMA((2,))],
        input_output_aliases={1: 0},
        compiler_params=params,
        cost_estimate=cost(0, 2),
        name="place",
    )(done, dual)
    return (dual.transpose(0, 2, 1, 3), gradient)


def solution(mesh):
    placed = (
        P("dir", "band", "space", None),
        P("dir", "band", "space", None),
        P("space", None),
        P("space", None),
        P(None, "band"),
        P("band"),
        P(),
        P("space", None),
    )
    return jax.shard_map(
        on_device,
        mesh=mesh,
        in_specs=placed,
        out_specs=(P("dir", "band", "space", None), P("space", None)),
        check_vma=False,
    )
```
